128 devices in a mesh: inst: 16 (over x, z), tp: 8 (over y, core).
Axes of the slice: x: 4, y: 4, z: 4, core: 2. Of those that a mesh axis runs over, the one named last changes fastest.
Arguments:
- queries: bfloat16 [4, 256, 64, 128], P(None, 'inst', 'tp'), may hold values from -6 to 6
- new_keys: bfloat16 [4, 256, 8, 128], P(None, 'inst', 'tp'), may hold values from -12 to 12
- new_values: bfloat16 [4, 256, 8, 128], P(None, 'inst', 'tp'), may hold values from -16 to 16
- key_pool: bfloat16 [2048, 8, 256, 128], P('inst', 'tp'), may hold values from -6 to 6
- value_pool: bfloat16 [2048, 8, 256, 128], P('inst', 'tp'), may hold values from -6 to 6
- block_table: int32 [2048], P('inst'), may hold values from 0 to 2047, as said below
- context_len: int32 [256], P('inst'), may hold values from 1 to 2048, 327680 in all
- out_weight: bfloat16 [8192, 8192], P('tp'), may hold values from -1 to 1
Outputs:
- projected: bfloat16 [4, 256, 8192], P(None, 'inst', 'tp')
The draws below stay inside these ranges and needn't reach their ends.
Inputs may be any that keep to these rules, and one draw needn't show every extreme that they name: `block_table`: a permutation of the slots: each slot holds exactly one block of one request; slot s lies with instance s // 128; every instance holds exactly 8 slots with blocks of the requests of each instance. `context_len`: at least one request has a full cache of 8 blocks.
All inputs are finite; a program needn't handle non-finite values.
Results may differ from the reference program's by a relative error of at most 0.0051.
Values may be sent and summed in bfloat16 or wider, within the bound.
No kernel may reach another device: no remote copies, remote signals or barrier semaphores. Data moves between devices by JAX's collectives and lax.ppermute only.
A program may use at most 128 MiB of HBM per device.

```python
import math
import jax
import jax.numpy as jnp
import numpy as np
from jax import lax

D = 8192
H = 64
KVH = 8
HEAD = 128
REQ = 16
MAXB = 8
DRAFT = 4
BLOCK = 256
REQS = 256
SLOTS = 2048
POOL = 128


def draw_queries(key, part):
    key = jax.random.fold_in(key, 3)
    first = jax.random.fold_in(key, 0)
    shape = (DRAFT, REQS, H, HEAD)
    result = jnp.clip(jax.random.normal(first, shape, jnp.float32), -6.0, 6.0)
    return result.astype(jnp.bfloat16)


def draw_key_pool(key, part):
    key = jax.random.fold_in(key, 5)
    first = jax.random.fold_in(key, 0)
    shape = (SLOTS, KVH, BLOCK, HEAD)
    result = jnp.clip(jax.random.normal(first, shape, jnp.float32), -6.0, 6.0)
    return result.astype(jnp.bfloat16)


def draw_block_table(key, part):
    key = jax.random.fold_in(key, 7)
    instances = REQS // REQ
    quota = POOL // instances
    owners = jnp.arange(instances, dtype=jnp.int32)

    def spread(index):
        return jax.random.permutation(jax.random.fold_in(key, index), POOL).astype(jnp.int32)

    def mixing(index):
        return jax.random.permutation(jax.random.fold_in(key, 100000 + index), POOL).astype(jnp.int32)
    chosen = jax.vmap(spread)(owners)
    lender = chosen // quota
    place = owners[:, None] * quota + chosen % quota
    mixes = jax.vmap(mixing)(owners)
    slots = lender * POOL + mixes[lender, place]
    return slots.reshape(SLOTS).astype(jnp.int32)


def level_of(stream_key, shape, cuts, smallest, top_value):
    def one(axis_at, shards_of):
        steps = jax.random.uniform(jax.random.fold_in(jax.random.fold_in(stream_key, 6), axis_at), (shards_of,), jnp.float32, smallest / len(cuts), top_value / len(cuts))
        return jnp.repeat(jnp.exp(steps), shape[axis_at] // shards_of).reshape((-1,) + (1,) * (len(shape) - axis_at - 1))

    gain = one(*cuts[0])
    for cut in cuts[1:]:
        gain = gain * one(*cut)
    return gain


def profile(amount, total, most, slope):
    weights = [(1 << 20) // math.isqrt(grade ** slope) + 1 for grade in range(2, amount + 1)]
    surplus, given = total - most - (amount - 1), [1] * (amount - 1)
    while surplus > 0:
        candidates = [i for i in range(amount - 1) if given[i] < most]
        pool, left = sum([weights[i] for i in candidates]), surplus
        for i in candidates:
            extra = min(most - given[i], max(1, left * weights[i] // pool), surplus)
            given[i] = given[i] + extra
            surplus = surplus - extra
    return np.array([most] + given)


def uneven(stream_key, count, total, bound, slope):
    if count == 2:
        one = jax.random.randint(stream_key, (), max(1, total - bound), min(bound, total - 1) + 1)
        return jnp.stack([one, total - one])
    sizes = jnp.asarray(profile(count, total, bound, slope), jnp.int32)
    pairs = (count - 1) // 2
    source_of, taker = sizes[1:1 + 2 * pairs:2], sizes[2:2 + 2 * pairs:2]
    room = jnp.minimum(source_of - 1, bound - taker)
    moved = jax.random.randint(jax.random.fold_in(stream_key, 1), (pairs,), 0, 1 << 20) % (room + 1)
    sizes = sizes.at[1:1 + 2 * pairs:2].set(source_of - moved).at[2:2 + 2 * pairs:2].set(taker + moved)
    return sizes[jax.random.permutation(jax.random.fold_in(stream_key, 2), count)]


def scatter_about(own_key, extent, deviation, most, cuts=(), kind=jnp.bfloat16):
    entries = jax.random.normal(own_key, extent, jnp.float32) * deviation
    if len(cuts) > 0:
        entries = level_of(own_key, extent, cuts, -0.22, 0.18) * entries
    return jnp.clip(entries, min=-most, max=most).astype(kind)


def setup_inputs(seed: int = 0) -> dict:
    key_list = jax.random.split(jax.random.key(seed), 9)
    queries = draw_queries(jax.random.fold_in(key_list[8], 71), 0)
    new_keys = scatter_about(key_list[1], (DRAFT, REQS, KVH, HEAD), 2.0, 12.0, ((1, 16), (2, 8)))
    new_values = scatter_about(key_list[2], (DRAFT, REQS, KVH, HEAD), 4.0, 16.0, ((1, 16), (2, 8)))
    key_pool = draw_key_pool(jax.random.fold_in(key_list[8], 71), 0)
    value_pool = scatter_about(key_list[4], (SLOTS, KVH, BLOCK, HEAD), 1.0, 6.0, ((0, 16), (1, 8)))
    block_table = draw_block_table(jax.random.fold_in(key_list[8], 71), 0)
    context_len = uneven(key_list[6], REQS, REQS * MAXB * BLOCK * 5 // 8, MAXB * BLOCK, 1).astype(jnp.int32)
    out_weight = scatter_about(key_list[7], (H * HEAD, D), (H * HEAD // 256) ** -0.5, 1.0, ((0, 8),))
    return {"queries": queries, "new_keys": new_keys, "new_values": new_values, "key_pool": key_pool, "value_pool": value_pool, "block_table": block_table, "context_len": context_len, "out_weight": out_weight}


NEG = -1e30


def reference(queries, new_keys, new_values, key_pool, value_pool, block_table, context_len, out_weight):
    group = H // KVH
    scale = HEAD ** -0.5
    causal = jnp.arange(DRAFT, dtype=jnp.int32)[None, :] <= jnp.arange(DRAFT, dtype=jnp.int32)[:, None]
    places = jnp.arange(MAXB, dtype=jnp.int32)[:, None] * BLOCK + jnp.arange(BLOCK, dtype=jnp.int32)[None, :]

    def one_request(index):
        slots = lax.dynamic_slice_in_dim(block_table, (index * MAXB).astype(jnp.int32), MAXB)
        keys = jnp.take(key_pool, slots, axis=0).astype(jnp.float32)
        values = jnp.take(value_pool, slots, axis=0).astype(jnp.float32)
        rows = lax.dynamic_index_in_dim(queries, index, 1, keepdims=False).astype(jnp.float32)
        rows = rows.reshape(DRAFT, KVH, group, HEAD)
        limit = lax.dynamic_index_in_dim(context_len, index, 0, keepdims=False)
        scores = jnp.einsum("dkgh,bkth->bkgdt", rows, keys) * scale
        valid = (places < limit)[:, None, None, None, :]
        peak = jnp.max(jnp.where(valid, scores, NEG), axis=-1)
        weights = jnp.exp(jnp.where(valid, scores - peak[..., None], NEG))
        total = jnp.sum(weights, axis=-1)
        rounded = lax.optimization_barrier(weights.astype(jnp.bfloat16)).astype(jnp.float32)
        summed = jnp.einsum("bkgdt,bkth->bkgdh", rounded, values)
        fresh_keys = lax.dynamic_index_in_dim(new_keys, index, 1, keepdims=False).astype(jnp.float32)
        fresh_values = lax.dynamic_index_in_dim(new_values, index, 1, keepdims=False).astype(jnp.float32)
        fresh = jnp.einsum("dkgh,ekh->kgde", rows, fresh_keys) * scale
        fresh_peak = jnp.max(jnp.where(causal, fresh, NEG), axis=-1)
        fresh_weights = jnp.exp(jnp.where(causal, fresh - fresh_peak[..., None], NEG))
        fresh_total = jnp.sum(fresh_weights, axis=-1)
        fresh_rounded = lax.optimization_barrier(fresh_weights.astype(jnp.bfloat16)).astype(jnp.float32)
        fresh_out = jnp.einsum("kgde,ekh->kgdh", fresh_rounded, fresh_values)
        top = jnp.maximum(jnp.max(peak, axis=0), fresh_peak)
        shift = jnp.exp(peak - top[None])
        fresh_shift = jnp.exp(fresh_peak - top)
        denom = jnp.sum(total * shift, axis=0) + fresh_total * fresh_shift
        numer = jnp.sum(summed * shift[..., None], axis=0) + fresh_out * fresh_shift[..., None]
        attended = (numer / denom[..., None]).astype(jnp.bfloat16)
        return attended.transpose(2, 0, 1, 3).reshape(DRAFT, H * HEAD)

    attended = lax.map(one_request, jnp.arange(REQS, dtype=jnp.int32))
    flat = attended.transpose(1, 0, 2).reshape(DRAFT * REQS, H * HEAD)
    product = jnp.dot(flat, out_weight, preferred_element_type=jnp.float32)
    return product.astype(jnp.bfloat16).reshape(DRAFT, REQS, D)
```

```python
import functools

import jax
import jax.numpy as jnp
from jax import lax
from jax.experimental import pallas as pl
from jax.experimental.pallas import tpu as pltpu
from jax.sharding import PartitionSpec as P

NEG = -1e30
F32 = jnp.float32
BF16 = jnp.bfloat16
META = 16


def prepare_kernel(table_ref, length_ref, q_ref, out_ref, place_ref, meta_ref, count_ref):
    lenders = out_ref.shape[0]
    rows = q_ref.shape[1]
    entries = table_ref.shape[0]
    pool = entries
    blocks = entries // q_ref.shape[0]
    each = entries // lenders
    block = 256

    def clear(i, _):
        count_ref[i] = 0
        return 0

    lax.fori_loop(0, lenders, clear, 0)

    def one(e, _):
        slot = table_ref[e]
        lender = slot // pool
        j = count_ref[lender]
        count_ref[lender] = j + 1
        place_ref[e] = lender * each + j
        r = e // blocks
        limit = jnp.clip(length_ref[r] - (e % blocks) * block, 0, block)
        out_ref[lender, pl.ds(pl.multiple_of(j * rows, rows), rows), :] = q_ref[r]
        lanes = (1, meta_ref.shape[2])
        meta_ref[lender, pl.ds(j, 1), :] = jnp.full(lanes, (slot % pool).astype(F32), F32)
        meta_ref[lender, pl.ds(each + j, 1), :] = jnp.full(lanes, limit.astype(F32), F32)
        return 0

    lax.fori_loop(0, entries, one, 0, unroll=8)
    out_ref[:, each * rows :, :] = meta_ref[...].astype(BF16)


def prepare(table, lengths, q):
    requests, rows, head = q.shape
    entries = table.shape[0]
    lenders = lax.axis_size("inst")
    each = entries // lenders
    return pl.pallas_call(
        prepare_kernel,
        in_specs=[
            pl.BlockSpec(memory_space=pltpu.SMEM),
            pl.BlockSpec(memory_space=pltpu.SMEM),
            pl.BlockSpec(memory_space=pltpu.VMEM),
        ],
        out_specs=[
            pl.BlockSpec(memory_space=pltpu.VMEM),
            pl.BlockSpec(memory_space=pltpu.SMEM),
        ],
        out_shape=[
            jax.ShapeDtypeStruct((lenders, each * rows + META, head), BF16),
            jax.ShapeDtypeStruct((entries,), jnp.int32),
        ],
        scratch_shapes=[
            pltpu.VMEM((lenders, META, head), F32),
            pltpu.SMEM((lenders,), jnp.int32),
        ],
        name="prepare",
    )(table, lengths, q)


def attend_kernel(rows, info_ref, q_ref, k_ref, v_ref, out_ref, stat_ref):
    step = pl.program_id(0)
    chunk = k_ref.shape[0]
    block, head = k_ref.shape[1:]
    lenders = out_ref.shape[0]
    each = (out_ref.shape[1] - META) // rows
    scale = head ** (-0.5)
    lane = lax.broadcasted_iota(jnp.int32, (rows, block), 1)
    column = lax.broadcasted_iota(jnp.int32, (rows, head), 1)

    entry = [info_ref[0, step * chunk + i] for i in range(chunk)]
    limit = [info_ref[1, step * chunk + i] for i in range(chunk)]
    at = [
        (entry[i] // each, pl.ds(pl.multiple_of((entry[i] % each) * rows, rows), rows))
        for i in range(chunk)
    ]
    scores = [
        lax.dot_general(
            q_ref[at[i][0], at[i][1], :],
            k_ref[i],
            (((1,), (1,)), ((), ())),
            preferred_element_type=F32,
        )
        for i in range(chunk)
    ]
    stat = stat_ref[...]
    for i in range(chunk):
        s = jnp.where(lane < limit[i], scores[i] * scale, NEG)
        peak = jnp.max(s, axis=1, keepdims=True)
        weight = jnp.exp(s - peak)
        total = jnp.sum(weight, axis=1, keepdims=True)
        summed = jnp.dot(weight.astype(BF16), v_ref[i], preferred_element_type=F32)
        out_ref[at[i][0], at[i][1], :] = (summed * (1.0 / total)).astype(BF16)
        lse = jnp.where(limit[i] > 0, peak + jnp.log(total), NEG)
        stat = jnp.where(column == entry[i], lse, stat)
    stat_ref[...] = stat

    @pl.when(step == pl.num_programs(0) - 1)
    def _():
        x = stat_ref[...]
        hi = x.astype(BF16).astype(F32)
        rest = x - hi
        mid = rest.astype(BF16).astype(F32)
        low = rest - mid
        stack = jnp.concatenate([hi, mid, low, jnp.zeros((head - 3 * rows, head), F32)], axis=0)
        turned = stack.T
        for i in range(lenders):
            part = jnp.concatenate(
                [turned[i * each : (i + 1) * each], jnp.zeros((META - each, head), F32)], axis=0
            )
            out_ref[i, each * rows :, :] = part.astype(BF16)


def attend(info, q, keys, values, rows, chunk):
    pool, block, head = keys.shape
    whole = pl.BlockSpec(q.shape, lambda i, info: (0, 0, 0))
    part = pl.BlockSpec((chunk, block, head), lambda i, info: (i, 0, 0))
    return pl.pallas_call(
        functools.partial(attend_kernel, rows),
        grid_spec=pltpu.PrefetchScalarGridSpec(
            num_scalar_prefetch=1,
            grid=(pool // chunk,),
            in_specs=[whole, part, part],
            out_specs=whole,
            scratch_shapes=[pltpu.VMEM((rows, pool), F32)],
        ),
        out_shape=jax.ShapeDtypeStruct(q.shape, BF16),
        compiler_params=pltpu.CompilerParams(vmem_limit_bytes=32 * 1024 * 1024),
        name="attend",
    )(info, q, keys, values)


def draft_kernel(drafts, q_ref, k_ref, v_ref, out_ref, lse_ref):
    requests, rows, head = q_ref.shape
    group = rows // drafts
    tall = requests * rows
    wide = k_ref.shape[0]
    q = q_ref[...].reshape(tall, head)
    s = lax.dot_general(q, k_ref[...], (((1,), (1,)), ((), ())), preferred_element_type=F32)
    s = s * head ** (-0.5)
    row = lax.broadcasted_iota(jnp.int32, (tall, wide), 0)
    col = lax.broadcasted_iota(jnp.int32, (tall, wide), 1)
    valid = (row // rows == col % requests) & (col // requests <= (row % rows) // group)
    s = jnp.where(valid, s, NEG)
    peak = jnp.max(s, axis=1, keepdims=True)
    weight = jnp.exp(s - peak)
    total = jnp.sum(weight, axis=1, keepdims=True)
    summed = jnp.dot(weight.astype(BF16), v_ref[...], preferred_element_type=F32)
    out_ref[...] = (summed * (1.0 / total)).reshape(requests, rows, head)
    lse = peak + jnp.log(total)
    row = lax.broadcasted_iota(jnp.int32, (tall, head), 0)
    lane = lax.broadcasted_iota(jnp.int32, (tall, head), 1)
    picked = jnp.where(row % rows == lane, lse, 0.0)
    lse_ref[...] = jnp.sum(picked.reshape(requests, rows, head), axis=1)


def draft_block(q, keys, values, drafts):
    requests, rows, head = q.shape
    vmem = pl.BlockSpec(memory_space=pltpu.VMEM)
    return pl.pallas_call(
        functools.partial(draft_kernel, drafts),
        in_specs=[vmem] * 3,
        out_specs=[vmem] * 2,
        out_shape=[
            jax.ShapeDtypeStruct((requests, rows, head), F32),
            jax.ShapeDtypeStruct((requests, head), F32),
        ],
        cost_estimate=pl.CostEstimate(flops=10**7, bytes_accessed=10**6, transcendentals=10**5),
        name="draft",
    )(q, keys, values)


def combine_kernel(
    drafts, place_ref, core_ref, got_ref, fresh_ref, fresh_lse_ref, w_ref,
    send_ref, att_ref, arrived_ref, own_ref, rows_ref,
):
    requests, rows, head = fresh_ref.shape
    lenders = got_ref.shape[0]
    entries = place_ref.shape[0]
    each = entries // lenders
    blocks = entries // requests
    group = rows // drafts

    @pl.when(pl.program_id(0) == 0)
    def _():
        for i in range(lenders):
            arrived_ref[i * each : (i + 1) * each, :] = got_ref[i, each * rows :, :].astype(F32)[
                :each
            ]
        for e in range(entries):
            own_ref[e : e + 1, :] = arrived_ref[pl.ds(place_ref[e], 1), :]
        x = own_ref[...]
        lse = x + pltpu.roll(x, head - rows, 1) + pltpu.roll(x, head - 2 * rows, 1)
        lse = lse.reshape(requests, blocks, head)
        fresh = fresh_lse_ref[...]
        top = jnp.maximum(jnp.max(lse, axis=1), fresh)
        weight = jnp.exp(lse - top[:, None])
        fresh_weight = jnp.exp(fresh - top)
        part = 1.0 / (jnp.sum(weight, axis=1) + fresh_weight)
        weight = (weight * part[:, None]).reshape(entries, head).T
        fresh_weight = (fresh_weight * part)
        fresh_weight = jnp.concatenate(
            [fresh_weight, jnp.zeros((head - requests, head), F32)], axis=0
        ).T
        for r in range(requests):
            acc = fresh_ref[r] * fresh_weight[:rows, r : r + 1]
            for b in range(blocks):
                e = r * blocks + b
                place = place_ref[e]
                block_out = got_ref[
                    place // each, pl.ds(pl.multiple_of((place % each) * rows, rows), rows), :
                ]
                acc += block_out.astype(F32) * weight[:rows, e : e + 1]
            for d in range(drafts):
                rows_ref[pl.ds((d * requests + r) * group, group), :] = acc[
                    d * group : (d + 1) * group
                ]
        att_ref[...] = jnp.concatenate(
            [rows_ref[pl.ds(g, drafts * requests, stride=group), :] for g in range(group)], axis=1
        ).astype(BF16)

    send_ref[0] = jnp.dot(att_ref[...], w_ref[...], preferred_element_type=F32).astype(BF16)


def combine(place, core, got, fresh, fresh_lse, w, drafts, tp):
    requests, rows, head = fresh.shape
    deep, wide = w.shape
    tile = wide // tp
    tall = drafts * requests

    def whole(x):
        return pl.BlockSpec(x.shape, lambda i, place, core: (0,) * x.ndim)

    return pl.pallas_call(
        functools.partial(combine_kernel, drafts),
        grid_spec=pltpu.PrefetchScalarGridSpec(
            num_scalar_prefetch=2,
            grid=(tp // 2,),
            in_specs=[
                whole(got),
                whole(fresh),
                whole(fresh_lse),
                pl.BlockSpec((deep, tile), lambda i, place, core: (0, 2 * i + 1 - core[0])),
            ],
            out_specs=[
                pl.BlockSpec((1, tall, tile), lambda i, place, core: (i, 0, 0)),
                pl.BlockSpec((tall, deep), lambda i, place, core: (0, 0)),
            ],
            scratch_shapes=[
                pltpu.VMEM((place.shape[0], head), F32),
                pltpu.VMEM((place.shape[0], head), F32),
                pltpu.VMEM((requests * rows, head), F32),
            ],
        ),
        out_shape=[
            jax.ShapeDtypeStruct((tp // 2, tall, tile), BF16),
            jax.ShapeDtypeStruct((tall, deep), BF16),
        ],
        compiler_params=pltpu.CompilerParams(vmem_limit_bytes=32 * 1024 * 1024),
        name="combine",
    )(place, core, got, fresh, fresh_lse, w)


def keep_kernel(core_ref, att_ref, w_ref, keep_ref):
    keep_ref[0] = jnp.dot(att_ref[...], w_ref[...], preferred_element_type=F32)


def keep_half(core, att, w, tp):
    deep, wide = w.shape
    tile = wide // tp
    tall = att.shape[0]
    return pl.pallas_call(
        keep_kernel,
        grid_spec=pltpu.PrefetchScalarGridSpec(
            num_scalar_prefetch=1,
            grid=(tp // 2,),
            in_specs=[
                pl.BlockSpec((tall, deep), lambda i, core: (0, 0)),
                pl.BlockSpec((deep, tile), lambda i, core: (0, 2 * i + core[0])),
            ],
            out_specs=pl.BlockSpec((1, tall, tile), lambda i, core: (i, 0, 0)),
        ),
        out_shape=jax.ShapeDtypeStruct((tp // 2, tall, tile), F32),
        compiler_params=pltpu.CompilerParams(vmem_limit_bytes=32 * 1024 * 1024),
        cost_estimate=pl.CostEstimate(
            flops=tall * deep * wide, bytes_accessed=deep * wide, transcendentals=0
        ),
        name="keep_half",
    )(core, att, w)


def on_device(
    queries, new_keys, new_values, key_pool, value_pool, block_table, context_len, out_weight
):
    drafts, requests, heads, head = queries.shape
    pool, _, block, _ = key_pool.shape
    tp = lax.axis_size("tp")
    rows = drafts * heads
    q = queries.transpose(1, 0, 2, 3).reshape(requests, rows, head)
    payload, place = prepare(block_table, context_len, q)
    asked = lax.all_to_all(payload, "inst", 0, 0, tiled=True)
    fresh, fresh_lse = draft_block(
        q, new_keys.reshape(-1, head), new_values.reshape(-1, head), drafts
    )

    each = pool // asked.shape[0]
    meta = asked[:, each * rows :, 0].astype(jnp.int32)
    slot = meta[:, :each].reshape(pool)
    limit = meta[:, each : 2 * each].reshape(pool)
    hit = slot[None, :] == jnp.arange(pool, dtype=jnp.int32)[:, None]
    numbers = jnp.stack([jnp.arange(pool, dtype=jnp.int32), limit])
    info = jnp.sum(jnp.where(hit[None], numbers[:, None, :], 0), axis=2)
    answer = attend(
        info, asked, key_pool.reshape(pool, block, head), value_pool.reshape(pool, block, head), rows, 16
    )
    got = lax.all_to_all(answer, "inst", 0, 0, tiled=True)

    core = (lax.axis_index("tp") % 2).astype(jnp.int32).reshape(1)
    send, att = combine(place, core, got, fresh, fresh_lse, out_weight, drafts, tp)
    other = lax.ppermute(send, "tp", [(i, i ^ 1) for i in range(tp)])
    keep = keep_half(core, att, out_weight, tp)
    pair = (keep + other.astype(F32)).astype(BF16)
    groups = [list(range(c, tp, 2)) for c in range(2)]
    parts = lax.all_to_all(pair, "tp", 0, 0, axis_index_groups=groups, tiled=True)
    result = jnp.sum(parts.astype(F32), axis=0).astype(BF16)
    return result.reshape(drafts, requests, -1)


def solution(mesh):
    return jax.shard_map(
        on_device,
        mesh=mesh,
        in_specs=(
            P(None, "inst", "tp", None),
            P(None, "inst", "tp", None),
            P(None, "inst", "tp", None),
            P("inst", "tp", None, None),
            P("inst", "tp", None, None),
            P("inst"),
            P("inst"),
            P("tp", None),
        ),
        out_specs=P(None, "inst", "tp"),
        check_vma=False,
    )
```

```python
import functools

import jax
import jax.numpy as jnp
from jax import lax
from jax.experimental import pallas as pl
from jax.experimental.pallas import tpu as pltpu
from jax.sharding import PartitionSpec as P

NEG = -1e30
F32 = jnp.float32
BF16 = jnp.bfloat16
META = 16


def in_hbm(x):
    return pltpu.with_memory_space_constraint(x, pltpu.HBM)


def draft_block(drafts, q, k_ref, v_ref, out_ref, stat_ref):
    requests, rows, head = q.shape
    group = rows // drafts
    tall = requests * rows
    wide = k_ref.shape[0]
    s = lax.dot_general(
        k_ref[...], q.reshape(tall, head), (((1,), (1,)), ((), ())), preferred_element_type=F32
    )
    key = lax.broadcasted_iota(jnp.int32, (wide, tall), 0)
    row = lax.broadcasted_iota(jnp.int32, (wide, tall), 1)
    request_bits, rows_bits, group_bits = (n.bit_length() - 1 for n in (requests, rows, group))
    own = lax.shift_right_logical(row, rows_bits) == (key & (requests - 1))
    drafted = lax.shift_right_logical(row & (rows - 1), group_bits)
    valid = own & (lax.shift_right_logical(key, request_bits) <= drafted)
    s = jnp.where(valid, s * head ** (-0.5), NEG)
    peak = jnp.max(s, axis=0, keepdims=True)
    weight = jnp.exp(s - peak)
    total = jnp.sum(weight, axis=0, keepdims=True)
    out_ref[...] = lax.dot_general(
        weight.astype(BF16), v_ref[...], (((0,), (0,)), ((), ())), preferred_element_type=F32
    ).reshape(requests, rows, head)
    for r in range(requests):
        start = r * rows // head * head
        for n, x in enumerate((peak, total)):
            piece = x[:, start : start + head]
            if r * rows > start:
                piece = pltpu.roll(piece, head - (r * rows - start), 1)
            stat_ref[n, r : r + 1, :] = piece


def prepare_kernel(
    shifts, table_hbm, length_hbm, queries_hbm, k_hbm, v_hbm,
    out_ref, place_ref, fresh_ref, stat_ref,
    table_ref, length_ref, queries_ref, k_ref, v_ref, q_ref, meta_ref, count_ref, sems,
):
    pairs = (
        (table_hbm, table_ref), (length_hbm, length_ref), (queries_hbm, queries_ref),
        (k_hbm, k_ref), (v_hbm, v_ref),
    )
    copies = [pltpu.make_async_copy(a, b, sems.at[i]) for i, (a, b) in enumerate(pairs)]
    for copy in copies:
        copy.start()
    drafts, requests, group, head = queries_ref.shape
    lenders = out_ref.shape[0]
    rows = drafts * group
    entries = table_ref.shape[0]
    each = entries // lenders
    pool_bits, blocks_bits, block_bits = shifts

    for i in range(lenders):
        count_ref[i] = 0
    for copy in copies:
        copy.wait()
    for r in range(requests):
        q_ref[r] = jnp.concatenate([queries_ref[d, r] for d in range(drafts)], axis=0)

    def one(e, _):
        slot = table_ref[e]
        lender = lax.shift_right_logical(slot, pool_bits)
        j = count_ref[lender]
        count_ref[lender] = j + 1
        place_ref[e] = lender * each + j
        r = lax.shift_right_logical(e, blocks_bits)
        start = lax.shift_left(e & ((1 << blocks_bits) - 1), block_bits)
        limit = jnp.clip(length_ref[r] - start, 0, 1 << block_bits)
        out_ref[lender, pl.ds(pl.multiple_of(j * rows, rows), rows), :] = q_ref[r]
        lanes = (1, head)
        inner = slot & ((1 << pool_bits) - 1)
        meta_ref[lender, pl.ds(j, 1), :] = jnp.full(lanes, inner.astype(F32), F32)
        meta_ref[lender, pl.ds(each + j, 1), :] = jnp.full(lanes, limit.astype(F32), F32)
        return 0

    lax.fori_loop(0, entries, one, 0, unroll=8)
    out_ref[:, each * rows :, :] = meta_ref[...].astype(BF16)
    draft_block(drafts, q_ref[...], k_ref, v_ref, fresh_ref, stat_ref)


def prepare(table, lengths, queries, new_keys, new_values, block):
    drafts, requests, group, head = queries.shape
    rows = drafts * group
    entries = table.shape[0]
    lenders = lax.axis_size("inst")
    each = entries // lenders
    shifts = tuple(n.bit_length() - 1 for n in (entries, entries // requests, block))
    vmem, smem = pl.BlockSpec(memory_space=pltpu.VMEM), pl.BlockSpec(memory_space=pltpu.SMEM)
    return pl.pallas_call(
        functools.partial(prepare_kernel, shifts),
        in_specs=[pl.BlockSpec(memory_space=pltpu.HBM)] * 5,
        out_specs=[vmem, smem, vmem, vmem],
        out_shape=[
            jax.ShapeDtypeStruct((lenders, each * rows + META, head), BF16),
            jax.ShapeDtypeStruct((entries,), jnp.int32),
            jax.ShapeDtypeStruct((requests, rows, head), F32),
            jax.ShapeDtypeStruct((2, requests, head), F32),
        ],
        scratch_shapes=[
            pltpu.SMEM(table.shape, jnp.int32),
            pltpu.SMEM(lengths.shape, jnp.int32),
            pltpu.VMEM(queries.shape, BF16),
            pltpu.VMEM(new_keys.shape, BF16),
            pltpu.VMEM(new_values.shape, BF16),
            pltpu.VMEM((requests, rows, head), BF16),
            pltpu.VMEM((lenders, META, head), F32),
            pltpu.SMEM((lenders,), jnp.int32),
            pltpu.SemaphoreType.DMA((5,)),
        ],
        compiler_params=pltpu.CompilerParams(vmem_limit_bytes=8 * 1024 * 1024),
        cost_estimate=pl.CostEstimate(
            flops=0, bytes_accessed=64 * 1024 * 1024, transcendentals=0
        ),
        name="prepare",
    )(*(in_hbm(x) for x in (table, lengths, queries, new_keys, new_values)))


def attend_kernel(rows, chunk, info_ref, q_ref, k_ref, v_ref, out_ref, stat_ref):
    block, head = k_ref.shape[1:]
    lenders = out_ref.shape[0]
    each = (out_ref.shape[1] - META) // rows
    scale = head ** (-0.5)
    lane = lax.broadcasted_iota(jnp.int32, (rows, block), 1)
    column = lax.broadcasted_iota(jnp.int32, (rows, head), 1)
    near = chunk // each

    def some(step, _):
        of = [(step * near + i // each, i % each) for i in range(chunk)]
        slot = [info_ref[n, j] for n, j in of]
        limit = [info_ref[n, each + j] for n, j in of]
        scores = [
            lax.dot_general(
                q_ref[n, j * rows : (j + 1) * rows, :],
                k_ref[slot[i]],
                (((1,), (1,)), ((), ())),
                preferred_element_type=F32,
            )
            for i, (n, j) in enumerate(of)
        ]
        stat = stat_ref[...]
        for i, (n, j) in enumerate(of):
            s = jnp.where(lane < limit[i], scores[i] * scale, NEG)
            peak = jnp.max(s, axis=1, keepdims=True)
            weight = jnp.exp(s - peak)
            total = jnp.sum(weight, axis=1, keepdims=True)
            summed = jnp.dot(weight.astype(BF16), v_ref[slot[i]], preferred_element_type=F32)
            out_ref[n, j * rows : (j + 1) * rows, :] = (summed * (1.0 / total)).astype(BF16)
            lse = jnp.where(limit[i] > 0, peak + jnp.log(total), NEG)
            stat = jnp.where(column == step * chunk + i, lse, stat)
        stat_ref[...] = stat
        return 0

    lax.fori_loop(0, lenders * each // chunk, some, 0)
    x = stat_ref[...]
    hi = x.astype(BF16).astype(F32)
    rest = x - hi
    mid = rest.astype(BF16).astype(F32)
    low = rest - mid
    stack = jnp.concatenate([hi, mid, low, jnp.zeros((head - 3 * rows, head), F32)], axis=0)
    turned = stack.T
    for i in range(lenders):
        part = jnp.concatenate(
            [turned[i * each : (i + 1) * each], jnp.zeros((META - each, head), F32)], axis=0
        )
        out_ref[i, each * rows :, :] = part.astype(BF16)


def attend(info, q, keys, values, rows, chunk):
    pool, block, head = keys.shape
    vmem, smem = pl.BlockSpec(memory_space=pltpu.VMEM), pl.BlockSpec(memory_space=pltpu.SMEM)
    return pl.pallas_call(
        functools.partial(attend_kernel, rows, chunk),
        in_specs=[smem, vmem, vmem, vmem],
        out_specs=vmem,
        out_shape=jax.ShapeDtypeStruct(q.shape, BF16),
        scratch_shapes=[pltpu.VMEM((rows, pool), F32)],
        compiler_params=pltpu.CompilerParams(vmem_limit_bytes=16 * 1024 * 1024),
        name="attend",
    )(info, q, keys, values)


def combine_kernel(
    drafts, place_ref, got_ref, fresh_ref, stat_ref, w_ref,
    send_ref, att_ref, arrived_ref, own_ref, rows_ref,
):
    requests, rows, head = fresh_ref.shape
    lenders = got_ref.shape[0]
    entries = place_ref.shape[0]
    each = entries // lenders
    each_bits = each.bit_length() - 1
    blocks = entries // requests
    group = rows // drafts

    for i in range(lenders):
        arrived_ref[i * each : (i + 1) * each, :] = got_ref[i, each * rows :, :].astype(F32)[:each]
    for e in range(entries):
        own_ref[e : e + 1, :] = arrived_ref[pl.ds(place_ref[e], 1), :]
    x = own_ref[...]
    lse = x + pltpu.roll(x, head - rows, 1) + pltpu.roll(x, head - 2 * rows, 1)
    lse = lse.reshape(requests, blocks, head)
    fresh_peak = stat_ref[0]
    top = jnp.maximum(jnp.max(lse, axis=1), fresh_peak)
    weight = jnp.exp(lse - top[:, None])
    fresh_weight = jnp.exp(fresh_peak - top)
    part = 1.0 / (jnp.sum(weight, axis=1) + stat_ref[1] * fresh_weight)
    weight = (weight * part[:, None]).reshape(entries, head).T
    fresh_weight = fresh_weight * part
    fresh_weight = jnp.concatenate(
        [fresh_weight, jnp.zeros((head - requests, head), F32)], axis=0
    ).T
    for r in range(requests):
        acc = fresh_ref[r] * fresh_weight[:rows, r : r + 1]
        for b in range(blocks):
            e = r * blocks + b
            place = place_ref[e]
            lender = lax.shift_right_logical(place, each_bits)
            start = pl.multiple_of((place & (each - 1)) * rows, rows)
            block_out = got_ref[lender, pl.ds(start, rows), :]
            acc += block_out.astype(F32) * weight[:rows, e : e + 1]
        for d in range(drafts):
            rows_ref[pl.ds((d * requests + r) * group, group), :] = acc[
                d * group : (d + 1) * group
            ]
    att = jnp.concatenate(
        [rows_ref[pl.ds(g, drafts * requests, stride=group), :] for g in range(group)], axis=1
    ).astype(BF16)
    att_ref[...] = att
    tile = send_ref.shape[2]
    place_tp = lax.axis_index("tp")
    core = place_tp & 1
    ring = send_ref.shape[0]
    for i in range(send_ref.shape[0]):
        to = ((place_tp >> 1) + i) & (ring - 1)
        here = pl.ds(pl.multiple_of((2 * to + 1 - core) * tile, tile), tile)
        send_ref[i] = jnp.dot(att, w_ref[:, here], preferred_element_type=F32).astype(BF16)


def combine(place, got, fresh, stat, w, drafts, tp):
    requests, rows, head = fresh.shape
    deep, wide = w.shape
    tile = wide // tp
    tall = drafts * requests
    vmem, smem = pl.BlockSpec(memory_space=pltpu.VMEM), pl.BlockSpec(memory_space=pltpu.SMEM)
    return pl.pallas_call(
        functools.partial(combine_kernel, drafts),
        in_specs=[smem, vmem, vmem, vmem, vmem],
        out_specs=[vmem, vmem],
        out_shape=[
            jax.ShapeDtypeStruct((tp // 2, tall, tile), BF16),
            jax.ShapeDtypeStruct((tall, deep), BF16),
        ],
        scratch_shapes=[
            pltpu.VMEM((place.shape[0], head), F32),
            pltpu.VMEM((place.shape[0], head), F32),
            pltpu.VMEM((requests * rows, head), F32),
        ],
        compiler_params=pltpu.CompilerParams(vmem_limit_bytes=16 * 1024 * 1024),
        name="combine",
    )(place, got, fresh, stat, w)


def keep_kernel(att_ref, w_ref, keep_ref):
    tile = keep_ref.shape[2]
    place_tp = lax.axis_index("tp")
    core = place_tp & 1
    ring = keep_ref.shape[0]
    for i in range(ring):
        to = ((place_tp >> 1) + i) & (ring - 1)
        here = pl.ds(pl.multiple_of((2 * to + core) * tile, tile), tile)
        keep_ref[i] = jnp.dot(att_ref[...], w_ref[:, here], preferred_element_type=F32)


def keep_half(att, w, tp):
    deep, wide = w.shape
    tile = wide // tp
    tall = att.shape[0]
    vmem, smem = pl.BlockSpec(memory_space=pltpu.VMEM), pl.BlockSpec(memory_space=pltpu.SMEM)
    return pl.pallas_call(
        keep_kernel,
        in_specs=[vmem, vmem],
        out_specs=vmem,
        out_shape=jax.ShapeDtypeStruct((tp // 2, tall, tile), F32),
        compiler_params=pltpu.CompilerParams(vmem_limit_bytes=16 * 1024 * 1024),
        cost_estimate=pl.CostEstimate(
            flops=tall * deep * wide, bytes_accessed=deep * wide, transcendentals=0
        ),
        name="keep_half",
    )(att, w)


def on_device(
    queries, new_keys, new_values, key_pool, value_pool, block_table, context_len, out_weight
):
    drafts, requests, heads, head = queries.shape
    pool, _, block, _ = key_pool.shape
    tp = lax.axis_size("tp")
    rows = drafts * heads
    payload, place, fresh, stat = prepare(
        block_table, context_len, queries, new_keys.reshape(-1, head), new_values.reshape(-1, head), block
    )
    asked = lax.all_to_all(payload, "inst", 0, 0, tiled=True)
    each = pool // asked.shape[0]
    info = asked[:, each * rows :, 0].astype(jnp.int32)
    answer = attend(
        info, asked, key_pool.reshape(pool, block, head), value_pool.reshape(pool, block, head), rows, 32
    )
    got = lax.all_to_all(answer, "inst", 0, 0, tiled=True)

    send, att = combine(place, got, fresh, stat, out_weight, drafts, tp)
    other = lax.ppermute(send, "tp", [(i, i ^ 1) for i in range(tp)])
    keep = keep_half(att, out_weight, tp)
    ring = tp // 2
    parts = [
        lax.ppermute(
            (keep[n] + other[n].astype(F32)).astype(BF16),
            "tp",
            [(i, (i + 2 * n) % tp) for i in range(tp)],
        )
        for n in range(1, ring)
    ]
    total = keep[0] + other[0].astype(F32)
    for part in parts:
        total = total + part.astype(F32)
    result = total.astype(BF16)
    return result.reshape(drafts, requests, -1)


def solution(mesh):
    return jax.shard_map(
        on_device,
        mesh=mesh,
        in_specs=(
            P(None, "inst", "tp", None),
            P(None, "inst", "tp", None),
            P(None, "inst", "tp", None),
            P("inst", "tp", None, None),
            P("inst", "tp", None, None),
            P("inst"),
            P("inst"),
            P("tp", None),
        ),
        out_specs=P(None, "inst", "tp"),
        check_vma=False,
    )
```

```python
import functools

import jax
import jax.numpy as jnp
from jax import lax
from jax.experimental import pallas as pl
from jax.experimental.pallas import tpu as pltpu
from jax.sharding import PartitionSpec as P

NEG = -1e30
F32 = jnp.float32
BF16 = jnp.bfloat16
META = 16


def in_hbm(x):
    return pltpu.with_memory_space_constraint(x, pltpu.HBM)


def draft_block(drafts, q, k_ref, v_ref, out_ref, stat_ref):
    requests, rows, head = q.shape
    group = rows // drafts
    tall = requests * rows
    wide = k_ref.shape[0]
    s = lax.dot_general(
        k_ref[...], q.reshape(tall, head), (((1,), (1,)), ((), ())), preferred_element_type=F32
    )
    key = lax.broadcasted_iota(jnp.int32, (wide, tall), 0)
    row = lax.broadcasted_iota(jnp.int32, (wide, tall), 1)
    request_bits, rows_bits, group_bits = (n.bit_length() - 1 for n in (requests, rows, group))
    own = lax.shift_right_logical(row, rows_bits) == (key & (requests - 1))
    drafted = lax.shift_right_logical(row & (rows - 1), group_bits)
    valid = own & (lax.shift_right_logical(key, request_bits) <= drafted)
    s = jnp.where(valid, s * head ** (-0.5), NEG)
    peak = jnp.max(s, axis=0, keepdims=True)
    weight = jnp.exp(s - peak)
    total = jnp.sum(weight, axis=0, keepdims=True)
    out_ref[...] = lax.dot_general(
        weight.astype(BF16), v_ref[...], (((0,), (0,)), ((), ())), preferred_element_type=F32
    ).reshape(requests, rows, head)
    for r in range(requests):
        start = r * rows // head * head
        for n, x in enumerate((peak, total)):
            piece = x[:, start : start + head]
            if r * rows > start:
                piece = pltpu.roll(piece, head - (r * rows - start), 1)
            stat_ref[n, r : r + 1, :] = piece


def prepare_kernel(
    shifts, table_hbm, length_hbm, queries_hbm, k_hbm, v_hbm,
    out_ref, place_ref, fresh_ref, stat_ref,
    table_ref, length_ref, queries_ref, k_ref, v_ref, q_ref, meta_ref, count_ref, sems,
):
    pairs = (
        (table_hbm, table_ref), (length_hbm, length_ref), (queries_hbm, queries_ref),
        (k_hbm, k_ref), (v_hbm, v_ref),
    )
    copies = [pltpu.make_async_copy(a, b, sems.at[i]) for i, (a, b) in enumerate(pairs)]
    for copy in copies:
        copy.start()
    drafts, requests, group, head = queries_ref.shape
    lenders = out_ref.shape[0]
    rows = drafts * group
    entries = table_ref.shape[0]
    each = entries // lenders
    pool_bits, blocks_bits, block_bits = shifts

    for i in range(lenders):
        count_ref[i] = 0
    for copy in copies:
        copy.wait()
    for r in range(requests):
        q_ref[r] = jnp.concatenate([queries_ref[d, r] for d in range(drafts)], axis=0)

    def one(e, _):
        slot = table_ref[e]
        lender = lax.shift_right_logical(slot, pool_bits)
        j = count_ref[lender]
        count_ref[lender] = j + 1
        place_ref[e] = lender * each + j
        r = lax.shift_right_logical(e, blocks_bits)
        start = lax.shift_left(e & ((1 << blocks_bits) - 1), block_bits)
        limit = jnp.clip(length_ref[r] - start, 0, 1 << block_bits)
        out_ref[lender, pl.ds(pl.multiple_of(j * rows, rows), rows), :] = q_ref[r]
        lanes = (1, head)
        inner = slot & ((1 << pool_bits) - 1)
        meta_ref[lender, pl.ds(j, 1), :] = jnp.full(lanes, inner.astype(F32), F32)
        meta_ref[lender, pl.ds(each + j, 1), :] = jnp.full(lanes, limit.astype(F32), F32)
        return 0

    lax.fori_loop(0, entries, one, 0, unroll=8)
    out_ref[:, each * rows :, :] = meta_ref[...].astype(BF16)
    draft_block(drafts, q_ref[...], k_ref, v_ref, fresh_ref, stat_ref)


def prepare(table, lengths, queries, new_keys, new_values, block):
    drafts, requests, group, head = queries.shape
    rows = drafts * group
    entries = table.shape[0]
    lenders = lax.axis_size("inst")
    each = entries // lenders
    shifts = tuple(n.bit_length() - 1 for n in (entries, entries // requests, block))
    vmem, smem = pl.BlockSpec(memory_space=pltpu.VMEM), pl.BlockSpec(memory_space=pltpu.SMEM)
    return pl.pallas_call(
        functools.partial(prepare_kernel, shifts),
        in_specs=[pl.BlockSpec(memory_space=pltpu.HBM)] * 5,
        out_specs=[vmem, smem, vmem, vmem],
        out_shape=[
            jax.ShapeDtypeStruct((lenders, each * rows + META, head), BF16),
            jax.ShapeDtypeStruct((entries,), jnp.int32),
            jax.ShapeDtypeStruct((requests, rows, head), F32),
            jax.ShapeDtypeStruct((2, requests, head), F32),
        ],
        scratch_shapes=[
            pltpu.SMEM(table.shape, jnp.int32),
            pltpu.SMEM(lengths.shape, jnp.int32),
            pltpu.VMEM(queries.shape, BF16),
            pltpu.VMEM(new_keys.shape, BF16),
            pltpu.VMEM(new_values.shape, BF16),
            pltpu.VMEM((requests, rows, head), BF16),
            pltpu.VMEM((lenders, META, head), F32),
            pltpu.SMEM((lenders,), jnp.int32),
            pltpu.SemaphoreType.DMA((5,)),
        ],
        compiler_params=pltpu.CompilerParams(vmem_limit_bytes=8 * 1024 * 1024),
        cost_estimate=pl.CostEstimate(
            flops=2 * 10**10, bytes_accessed=64 * 1024 * 1024, transcendentals=10**7
        ),
        name="prepare",
    )(*(in_hbm(x) for x in (table, lengths, queries, new_keys, new_values)))


def attend_kernel(rows, chunk, info_ref, q_ref, k_ref, v_ref, out_ref, stat_ref):
    block, head = k_ref.shape[1:]
    lenders = out_ref.shape[0]
    each = (out_ref.shape[1] - META) // rows
    scale = head ** (-0.5)
    lane = lax.broadcasted_iota(jnp.int32, (rows, block), 1)
    column = lax.broadcasted_iota(jnp.int32, (rows, head), 1)
    near = chunk // each

    def some(step, _):
        of = [(step * near + i // each, i % each) for i in range(chunk)]
        slot = [info_ref[n, j] for n, j in of]
        limit = [info_ref[n, each + j] for n, j in of]
        scores = [
            lax.dot_general(
                q_ref[n, j * rows : (j + 1) * rows, :],
                k_ref[slot[i]],
                (((1,), (1,)), ((), ())),
                preferred_element_type=F32,
            )
            for i, (n, j) in enumerate(of)
        ]
        stat = stat_ref[...]
        for i, (n, j) in enumerate(of):
            s = jnp.where(lane < limit[i], scores[i] * scale, NEG)
            peak = jnp.max(s, axis=1, keepdims=True)
            weight = jnp.exp(s - peak)
            total = jnp.sum(weight, axis=1, keepdims=True)
            summed = jnp.dot(weight.astype(BF16), v_ref[slot[i]], preferred_element_type=F32)
            out_ref[n, j * rows : (j + 1) * rows, :] = (summed * (1.0 / total)).astype(BF16)
            lse = jnp.where(limit[i] > 0, peak + jnp.log(total), NEG)
            stat = jnp.where(column == step * chunk + i, lse, stat)
        stat_ref[...] = stat
        return 0

    lax.fori_loop(0, lenders * each // chunk, some, 0)
    x = stat_ref[...]
    hi = x.astype(BF16).astype(F32)
    rest = x - hi
    mid = rest.astype(BF16).astype(F32)
    low = rest - mid
    stack = jnp.concatenate([hi, mid, low, jnp.zeros((head - 3 * rows, head), F32)], axis=0)
    turned = stack.T
    for i in range(lenders):
        part = jnp.concatenate(
            [turned[i * each : (i + 1) * each], jnp.zeros((META - each, head), F32)], axis=0
        )
        out_ref[i, each * rows :, :] = part.astype(BF16)


def attend(info, q, keys, values, rows, chunk):
    pool, block, head = keys.shape
    vmem, smem = pl.BlockSpec(memory_space=pltpu.VMEM), pl.BlockSpec(memory_space=pltpu.SMEM)
    return pl.pallas_call(
        functools.partial(attend_kernel, rows, chunk),
        in_specs=[smem, vmem, vmem, vmem],
        out_specs=vmem,
        out_shape=jax.ShapeDtypeStruct(q.shape, BF16),
        scratch_shapes=[pltpu.VMEM((rows, pool), F32)],
        compiler_params=pltpu.CompilerParams(vmem_limit_bytes=16 * 1024 * 1024),
        name="attend",
    )(info, q, keys, values)


def combine_kernel(
    drafts, place_ref, got_ref, fresh_ref, stat_ref, w_ref,
    send_ref, att_ref, arrived_ref, own_ref, rows_ref,
):
    requests, rows, head = fresh_ref.shape
    lenders = got_ref.shape[0]
    entries = place_ref.shape[0]
    each = entries // lenders
    each_bits = each.bit_length() - 1
    blocks = entries // requests
    group = rows // drafts

    for i in range(lenders):
        arrived_ref[i * each : (i + 1) * each, :] = got_ref[i, each * rows :, :].astype(F32)[:each]
    for e in range(entries):
        own_ref[e : e + 1, :] = arrived_ref[pl.ds(place_ref[e], 1), :]
    x = own_ref[...]
    lse = x + pltpu.roll(x, head - rows, 1) + pltpu.roll(x, head - 2 * rows, 1)
    lse = lse.reshape(requests, blocks, head)
    fresh_peak = stat_ref[0]
    top = jnp.maximum(jnp.max(lse, axis=1), fresh_peak)
    weight = jnp.exp(lse - top[:, None])
    fresh_weight = jnp.exp(fresh_peak - top)
    part = 1.0 / (jnp.sum(weight, axis=1) + stat_ref[1] * fresh_weight)
    weight = (weight * part[:, None]).reshape(entries, head).T
    fresh_weight = fresh_weight * part
    fresh_weight = jnp.concatenate(
        [fresh_weight, jnp.zeros((head - requests, head), F32)], axis=0
    ).T
    for r in range(requests):
        acc = fresh_ref[r] * fresh_weight[:rows, r : r + 1]
        for b in range(blocks):
            e = r * blocks + b
            place = place_ref[e]
            lender = lax.shift_right_logical(place, each_bits)
            start = pl.multiple_of((place & (each - 1)) * rows, rows)
            block_out = got_ref[lender, pl.ds(start, rows), :]
            acc += block_out.astype(F32) * weight[:rows, e : e + 1]
        for d in range(drafts):
            rows_ref[pl.ds((d * requests + r) * group, group), :] = acc[
                d * group : (d + 1) * group
            ]
    att = jnp.concatenate(
        [rows_ref[pl.ds(g, drafts * requests, stride=group), :] for g in range(group)], axis=1
    ).astype(BF16)
    att_ref[...] = att
    tile = send_ref.shape[2]
    place_tp = lax.axis_index("tp")
    core = place_tp & 1
    ring = send_ref.shape[0]
    for i in range(send_ref.shape[0]):
        to = ((place_tp >> 1) + i) & (ring - 1)
        here = pl.ds(pl.multiple_of((2 * to + 1 - core) * tile, tile), tile)
        send_ref[i] = jnp.dot(att, w_ref[:, here], preferred_element_type=F32).astype(BF16)


def combine(place, got, fresh, stat, w, drafts, tp):
    requests, rows, head = fresh.shape
    deep, wide = w.shape
    tile = wide // tp
    tall = drafts * requests
    vmem, smem = pl.BlockSpec(memory_space=pltpu.VMEM), pl.BlockSpec(memory_space=pltpu.SMEM)
    return pl.pallas_call(
        functools.partial(combine_kernel, drafts),
        in_specs=[smem, vmem, vmem, vmem, vmem],
        out_specs=[vmem, vmem],
        out_shape=[
            jax.ShapeDtypeStruct((tp // 2, tall, tile), BF16),
            jax.ShapeDtypeStruct((tall, deep), BF16),
        ],
        scratch_shapes=[
            pltpu.VMEM((place.shape[0], head), F32),
            pltpu.VMEM((place.shape[0], head), F32),
            pltpu.VMEM((requests * rows, head), F32),
        ],
        compiler_params=pltpu.CompilerParams(vmem_limit_bytes=16 * 1024 * 1024),
        name="combine",
    )(place, got, fresh, stat, w)


def keep_kernel(att_ref, w_ref, keep_ref):
    tile = keep_ref.shape[2]
    place_tp = lax.axis_index("tp")
    core = place_tp & 1
    ring = keep_ref.shape[0]
    for i in range(ring):
        to = ((place_tp >> 1) + i) & (ring - 1)
        here = pl.ds(pl.multiple_of((2 * to + core) * tile, tile), tile)
        keep_ref[i] = jnp.dot(att_ref[...], w_ref[:, here], preferred_element_type=F32)


def keep_half(att, w, tp):
    deep, wide = w.shape
    tile = wide // tp
    tall = att.shape[0]
    vmem, smem = pl.BlockSpec(memory_space=pltpu.VMEM), pl.BlockSpec(memory_space=pltpu.SMEM)
    return pl.pallas_call(
        keep_kernel,
        in_specs=[vmem, vmem],
        out_specs=vmem,
        out_shape=jax.ShapeDtypeStruct((tp // 2, tall, tile), F32),
        compiler_params=pltpu.CompilerParams(vmem_limit_bytes=16 * 1024 * 1024),
        cost_estimate=pl.CostEstimate(
            flops=tall * deep * wide, bytes_accessed=deep * wide, transcendentals=0
        ),
        name="keep_half",
    )(att, w)


def on_device(
    queries, new_keys, new_values, key_pool, value_pool, block_table, context_len, out_weight
):
    drafts, requests, heads, head = queries.shape
    pool, _, block, _ = key_pool.shape
    tp = lax.axis_size("tp")
    rows = drafts * heads
    payload, place, fresh, stat = prepare(
        block_table, context_len, queries, new_keys.reshape(-1, head), new_values.reshape(-1, head), block
    )
    asked = lax.all_to_all(payload, "inst", 0, 0, tiled=True)
    each = pool // asked.shape[0]
    info = asked[:, each * rows :, 0].astype(jnp.int32)
    answer = attend(
        info, asked, key_pool.reshape(pool, block, head), value_pool.reshape(pool, block, head), rows, 32
    )
    got = lax.all_to_all(answer, "inst", 0, 0, tiled=True)

    send, att = combine(place, got, fresh, stat, out_weight, drafts, tp)
    other = lax.ppermute(send, "tp", [(i, i ^ 1) for i in range(tp)])
    keep = keep_half(att, out_weight, tp)
    ring = tp // 2
    parts = [
        lax.ppermute(
            (keep[n] + other[n].astype(F32)).astype(BF16),
            "tp",
            [(i, (i + 2 * n) % tp) for i in range(tp)],
        )
        for n in range(1, ring)
    ]
    total = keep[0] + other[0].astype(F32)
    for part in parts:
        total = total + part.astype(F32)
    result = total.astype(BF16)
    return result.reshape(drafts, requests, -1)


def solution(mesh):
    return jax.shard_map(
        on_device,
        mesh=mesh,
        in_specs=(
            P(None, "inst", "tp", None),
            P(None, "inst", "tp", None),
            P(None, "inst", "tp", None),
            P("inst", "tp", None, None),
            P("inst", "tp", None, None),
            P("inst"),
            P("inst"),
            P("tp", None),
        ),
        out_specs=P(None, "inst", "tp"),
        check_vma=False,
    )
```

```python
import functools
import math

import jax
import jax.numpy as jnp
from jax import lax
from jax.experimental import pallas as pl
from jax.experimental.pallas import tpu as pltpu
from jax.sharding import PartitionSpec as P

NEG = -1e30
F32 = jnp.float32
BF16 = jnp.bfloat16
META = 16


def in_hbm(x):
    return pltpu.with_memory_space_constraint(x, pltpu.HBM)


def draft_block(drafts, q, k_ref, v_ref, out_ref, stat_ref):
    requests, rows, head = q.shape
    group = rows // drafts
    tall = requests * rows
    wide = k_ref.shape[0]
    s = lax.dot_general(
        k_ref[...], q.reshape(tall, head), (((1,), (1,)), ((), ())), preferred_element_type=F32
    )
    key = lax.broadcasted_iota(jnp.int32, (wide, tall), 0)
    row = lax.broadcasted_iota(jnp.int32, (wide, tall), 1)
    request_bits, rows_bits, group_bits = (n.bit_length() - 1 for n in (requests, rows, group))
    own = lax.shift_right_logical(row, rows_bits) == (key & (requests - 1))
    drafted = lax.shift_right_logical(row & (rows - 1), group_bits)
    valid = own & (lax.shift_right_logical(key, request_bits) <= drafted)
    s = jnp.where(valid, s * head ** (-0.5), NEG)
    peak = jnp.max(s, axis=0, keepdims=True)
    weight = jnp.exp(s - peak)
    total = jnp.sum(weight, axis=0, keepdims=True)
    out_ref[...] = lax.dot_general(
        weight.astype(BF16), v_ref[...], (((0,), (0,)), ((), ())), preferred_element_type=F32
    ).reshape(requests, rows, head)
    for r in range(requests):
        start = r * rows // head * head
        for n, x in enumerate((peak, total)):
            piece = x[:, start : start + head]
            if r * rows > start:
                piece = pltpu.roll(piece, head - (r * rows - start), 1)
            stat_ref[n, r : r + 1, :] = piece


def prepare_kernel(
    shifts, table_hbm, length_hbm, queries_hbm, k_hbm, v_hbm,
    out_ref, place_ref, fresh_ref, stat_ref,
    table_ref, length_ref, queries_ref, k_ref, v_ref, q_ref, meta_ref, count_ref, sems,
):
    pairs = (
        (table_hbm, table_ref), (length_hbm, length_ref), (queries_hbm, queries_ref),
        (k_hbm, k_ref), (v_hbm, v_ref),
    )
    copies = [pltpu.make_async_copy(a, b, sems.at[i]) for i, (a, b) in enumerate(pairs)]
    for copy in copies:
        copy.start()
    drafts, requests, group, head = queries_ref.shape
    lenders = out_ref.shape[0]
    rows = drafts * group
    entries = table_ref.shape[0]
    each = entries // lenders
    pool_bits, blocks_bits, block_bits = shifts

    for i in range(lenders):
        count_ref[i] = 0
    for copy in copies:
        copy.wait()
    for r in range(requests):
        q_ref[r] = jnp.concatenate([queries_ref[d, r] for d in range(drafts)], axis=0)

    def one(e, _):
        slot = table_ref[e]
        lender = lax.shift_right_logical(slot, pool_bits)
        j = count_ref[lender]
        count_ref[lender] = j + 1
        place_ref[e] = lender * each + j
        r = lax.shift_right_logical(e, blocks_bits)
        start = lax.shift_left(e & ((1 << blocks_bits) - 1), block_bits)
        limit = jnp.clip(length_ref[r] - start, 0, 1 << block_bits)
        out_ref[lender, pl.ds(pl.multiple_of(j * rows, rows), rows), :] = q_ref[r]
        lanes = (1, head)
        inner = slot & ((1 << pool_bits) - 1)
        meta_ref[lender, pl.ds(j, 1), :] = jnp.full(lanes, inner.astype(F32), F32)
        meta_ref[lender, pl.ds(each + j, 1), :] = jnp.full(lanes, limit.astype(F32), F32)
        return 0

    lax.fori_loop(0, entries, one, 0, unroll=True)
    out_ref[:, each * rows :, :] = meta_ref[...].astype(BF16)
    draft_block(drafts, q_ref[...], k_ref, v_ref, fresh_ref, stat_ref)


def prepare(table, lengths, queries, new_keys, new_values, block):
    drafts, requests, group, head = queries.shape
    rows = drafts * group
    entries = table.shape[0]
    lenders = lax.axis_size("inst")
    each = entries // lenders
    shifts = tuple(n.bit_length() - 1 for n in (entries, entries // requests, block))
    vmem, smem = pl.BlockSpec(memory_space=pltpu.VMEM), pl.BlockSpec(memory_space=pltpu.SMEM)
    return pl.pallas_call(
        functools.partial(prepare_kernel, shifts),
        in_specs=[pl.BlockSpec(memory_space=pltpu.HBM)] * 5,
        out_specs=[vmem, smem, vmem, vmem],
        out_shape=[
            jax.ShapeDtypeStruct((lenders, each * rows + META, head), BF16),
            jax.ShapeDtypeStruct((entries,), jnp.int32),
            jax.ShapeDtypeStruct((requests, rows, head), F32),
            jax.ShapeDtypeStruct((2, requests, head), F32),
        ],
        scratch_shapes=[
            pltpu.SMEM(table.shape, jnp.int32),
            pltpu.SMEM(lengths.shape, jnp.int32),
            pltpu.VMEM(queries.shape, BF16),
            pltpu.VMEM(new_keys.shape, BF16),
            pltpu.VMEM(new_values.shape, BF16),
            pltpu.VMEM((requests, rows, head), BF16),
            pltpu.VMEM((lenders, META, head), F32),
            pltpu.SMEM((lenders,), jnp.int32),
            pltpu.SemaphoreType.DMA((5,)),
        ],
        compiler_params=pltpu.CompilerParams(vmem_limit_bytes=8 * 1024 * 1024),
        cost_estimate=pl.CostEstimate(
            flops=2 * 10**10, bytes_accessed=64 * 1024 * 1024, transcendentals=10**7
        ),
        name="prepare",
    )(*(in_hbm(x) for x in (table, lengths, queries, new_keys, new_values)))


def attend_kernel(
    rows, ahead, behind, q_ref, k_ref, v_ref, out_ref, number_ref, info_ref, sem
):
    block, head = k_ref.shape[1:]
    lenders = out_ref.shape[0]
    each = (out_ref.shape[1] - META) // rows
    entries = lenders * each
    scale = head ** (-0.5)
    fast = scale * math.log2(math.e)

    lane = lax.broadcasted_iota(jnp.int32, (META, head), 1)
    row = lax.broadcasted_iota(jnp.int32, (META, head), 0)
    for n in range(lenders):
        meta = jnp.where(lane == row, q_ref[n, each * rows :, :].astype(F32), 0.0)
        number_ref[n : n + 1, :] = jnp.sum(meta, axis=0, keepdims=True).astype(jnp.int32)
    copy = pltpu.make_async_copy(number_ref, info_ref, sem)
    copy.start()
    copy.wait()

    token = lax.broadcasted_iota(jnp.int32, (8, block), 1)
    column = lax.broadcasted_iota(jnp.int32, (rows, head), 1)
    slot = [info_ref[i // each, i % each] for i in range(entries)]
    limit = [info_ref[i // each, each + i % each] for i in range(entries)]

    def here(i):
        return i // each, pl.ds(i % each * rows, rows), slice(None)

    scores, soft, outs = {}, {}, {}
    peaks = jnp.zeros((rows, head), F32)
    totals = jnp.ones((rows, head), F32)
    for i in range(-ahead, entries + 2 * behind):
        if i + ahead < entries:
            n = i + ahead
            scores[n] = lax.dot_general(
                q_ref[here(n)],
                k_ref[slot[n]],
                (((1,), (1,)), ((), ())),
                preferred_element_type=F32,
            )
        if 0 <= i < entries:
            bias = jnp.where(token < limit[i], 0.0, NEG)
            s = scores.pop(i).reshape(rows // 8, 8, block) + bias[None]
            s = s.reshape(rows, block)
            peak = jnp.max(s, axis=1, keepdims=True)
            weight = jnp.exp2((s - peak) * fast)
            soft[i] = peak, jnp.sum(weight, axis=1, keepdims=True), weight.astype(BF16)
        if 0 <= i - behind < entries:
            n = i - behind
            outs[n] = jnp.dot(soft[n][2], v_ref[slot[n]], preferred_element_type=F32)
        if 0 <= i - 2 * behind < entries:
            n = i - 2 * behind
            peak, total, _ = soft.pop(n)
            out_ref[here(n)] = (outs.pop(n) * (1.0 / total)).astype(BF16)
            peaks = jnp.where(column == n, peak, peaks)
            totals = jnp.where(column == n, total, totals)

    x = peaks * scale + jnp.log(totals)
    hi = x.astype(BF16).astype(F32)
    rest = x - hi
    mid = rest.astype(BF16).astype(F32)
    low = rest - mid
    stack = jnp.concatenate([hi, mid, low, jnp.zeros((head - 3 * rows, head), F32)], axis=0)
    turned = stack.T
    for i in range(lenders):
        part = jnp.concatenate(
            [turned[i * each : (i + 1) * each], jnp.zeros((META - each, head), F32)], axis=0
        )
        out_ref[i, each * rows :, :] = part.astype(BF16)


def attend(q, keys, values, rows):
    lenders = q.shape[0]
    head = q.shape[2]
    vmem = pl.BlockSpec(memory_space=pltpu.VMEM)
    return pl.pallas_call(
        functools.partial(attend_kernel, rows, 8, 4),
        in_specs=[vmem, vmem, vmem],
        out_specs=vmem,
        out_shape=jax.ShapeDtypeStruct(q.shape, BF16),
        scratch_shapes=[
            pltpu.VMEM((lenders, head), jnp.int32),
            pltpu.SMEM((lenders, head), jnp.int32),
            pltpu.SemaphoreType.DMA,
        ],
        compiler_params=pltpu.CompilerParams(vmem_limit_bytes=16 * 1024 * 1024),
        name="attend",
    )(q, keys, values)


def combine_kernel(
    drafts, place_ref, got_ref, fresh_ref, stat_ref, w_ref,
    send_ref, att_ref, arrived_ref, own_ref, rows_ref,
):
    requests, rows, head = fresh_ref.shape
    lenders = got_ref.shape[0]
    entries = place_ref.shape[0]
    each = entries // lenders
    each_bits = each.bit_length() - 1
    blocks = entries // requests
    group = rows // drafts

    for i in range(lenders):
        arrived_ref[i * each : (i + 1) * each, :] = got_ref[i, each * rows :, :].astype(F32)[:each]
    for e in range(entries):
        own_ref[e : e + 1, :] = arrived_ref[pl.ds(place_ref[e], 1), :]
    x = own_ref[...]
    lse = x + pltpu.roll(x, head - rows, 1) + pltpu.roll(x, head - 2 * rows, 1)
    lse = lse.reshape(requests, blocks, head)
    fresh_peak = stat_ref[0]
    top = jnp.maximum(jnp.max(lse, axis=1), fresh_peak)
    weight = jnp.exp(lse - top[:, None])
    fresh_weight = jnp.exp(fresh_peak - top)
    part = 1.0 / (jnp.sum(weight, axis=1) + stat_ref[1] * fresh_weight)
    lane = lax.broadcasted_iota(jnp.int32, (entries, head), 1)
    weight = jnp.where(lane < rows, (weight * part[:, None]).reshape(entries, head), 0.0)
    fresh_weight = fresh_weight * part
    fresh_weight = jnp.concatenate(
        [fresh_weight, jnp.zeros((head - requests, head), F32)], axis=0
    ).T
    beside = head // rows
    rows_bits = rows.bit_length() - 1
    spread = weight
    for n in range(1, beside):
        spread = spread + pltpu.roll(weight, n * rows, 1)
    lane = lax.broadcasted_iota(jnp.int32, (blocks, head), 1)
    near = lax.broadcasted_iota(jnp.int32, (blocks, head), 0) - lax.shift_right_logical(
        lane, rows_bits
    )
    diagonal = lax.broadcasted_iota(jnp.int32, (rows, head), 0) == (
        lax.broadcasted_iota(jnp.int32, (rows, head), 1) & (rows - 1)
    )
    for r in range(requests):
        mine = spread[r * blocks : (r + 1) * blocks]
        high, low, parts = [], [], []
        for n in range(0, blocks, beside):
            line = jnp.sum(jnp.where(near == n, mine, 0.0), axis=0, keepdims=True)
            square = jnp.where(diagonal, line, 0.0)
            high.append(square.astype(BF16))
            low.append((square - high[-1].astype(F32)).astype(BF16))
        for b in range(blocks):
            place = place_ref[r * blocks + b]
            lender = lax.shift_right_logical(place, each_bits)
            start = pl.multiple_of((place & (each - 1)) * rows, rows)
            parts.append(got_ref[lender, pl.ds(start, rows), :])
        left = jnp.concatenate(
            [jnp.concatenate(high, axis=1), jnp.concatenate(low, axis=1)], axis=0
        )
        both = jnp.dot(left, jnp.concatenate(parts, axis=0), preferred_element_type=F32)
        acc = both[:rows] + both[rows:] + fresh_ref[r] * fresh_weight[:rows, r : r + 1]
        for d in range(drafts):
            rows_ref[pl.ds((d * requests + r) * group, group), :] = acc[
                d * group : (d + 1) * group
            ]
    att = jnp.concatenate(
        [rows_ref[pl.ds(g, drafts * requests, stride=group), :] for g in range(group)], axis=1
    ).astype(BF16)
    att_ref[...] = att
    tile = send_ref.shape[2]
    place_tp = lax.axis_index("tp")
    core = place_tp & 1
    ring = send_ref.shape[0]
    for i in range(send_ref.shape[0]):
        to = ((place_tp >> 1) + i) & (ring - 1)
        here = pl.ds(pl.multiple_of((2 * to + 1 - core) * tile, tile), tile)
        send_ref[i] = jnp.dot(att, w_ref[:, here], preferred_element_type=F32).astype(BF16)


def combine(place, got, fresh, stat, w, drafts, tp):
    requests, rows, head = fresh.shape
    deep, wide = w.shape
    tile = wide // tp
    tall = drafts * requests
    vmem, smem = pl.BlockSpec(memory_space=pltpu.VMEM), pl.BlockSpec(memory_space=pltpu.SMEM)
    return pl.pallas_call(
        functools.partial(combine_kernel, drafts),
        in_specs=[smem, vmem, vmem, vmem, vmem],
        out_specs=[vmem, vmem],
        out_shape=[
            jax.ShapeDtypeStruct((tp // 2, tall, tile), BF16),
            jax.ShapeDtypeStruct((tall, deep), BF16),
        ],
        scratch_shapes=[
            pltpu.VMEM((place.shape[0], head), F32),
            pltpu.VMEM((place.shape[0], head), F32),
            pltpu.VMEM((requests * rows, head), F32),
        ],
        compiler_params=pltpu.CompilerParams(vmem_limit_bytes=16 * 1024 * 1024),
        name="combine",
    )(place, got, fresh, stat, w)


def keep_kernel(att_ref, w_ref, keep_ref):
    tile = keep_ref.shape[2]
    place_tp = lax.axis_index("tp")
    core = place_tp & 1
    ring = keep_ref.shape[0]
    for i in range(ring):
        to = ((place_tp >> 1) + i) & (ring - 1)
        here = pl.ds(pl.multiple_of((2 * to + core) * tile, tile), tile)
        keep_ref[i] = jnp.dot(att_ref[...], w_ref[:, here], preferred_element_type=F32)


def keep_half(att, w, tp):
    deep, wide = w.shape
    tile = wide // tp
    tall = att.shape[0]
    vmem, smem = pl.BlockSpec(memory_space=pltpu.VMEM), pl.BlockSpec(memory_space=pltpu.SMEM)
    return pl.pallas_call(
        keep_kernel,
        in_specs=[vmem, vmem],
        out_specs=vmem,
        out_shape=jax.ShapeDtypeStruct((tp // 2, tall, tile), F32),
        compiler_params=pltpu.CompilerParams(vmem_limit_bytes=16 * 1024 * 1024),
        cost_estimate=pl.CostEstimate(
            flops=tall * deep * wide, bytes_accessed=deep * wide, transcendentals=0
        ),
        name="keep_half",
    )(att, w)


def on_device(
    queries, new_keys, new_values, key_pool, value_pool, block_table, context_len, out_weight
):
    drafts, requests, heads, head = queries.shape
    pool, _, block, _ = key_pool.shape
    tp = lax.axis_size("tp")
    rows = drafts * heads
    payload, place, fresh, stat = prepare(
        block_table, context_len, queries, new_keys.reshape(-1, head), new_values.reshape(-1, head), block
    )
    asked = lax.all_to_all(payload, "inst", 0, 0, tiled=True)
    answer = attend(
        asked, key_pool.reshape(pool, block, head), value_pool.reshape(pool, block, head), rows
    )
    got = lax.all_to_all(answer, "inst", 0, 0, tiled=True)

    send, att = combine(place, got, fresh, stat, out_weight, drafts, tp)
    other = lax.ppermute(send, "tp", [(i, i ^ 1) for i in range(tp)])
    keep = keep_half(att, out_weight, tp)
    ring = tp // 2
    parts = [
        lax.ppermute(
            (keep[n] + other[n].astype(F32)).astype(BF16),
            "tp",
            [(i, (i + 2 * n) % tp) for i in range(tp)],
        )
        for n in (2, 1, 3)
    ]
    total = keep[0] + other[0].astype(F32)
    for part in parts:
        total = total + part.astype(F32)
    result = total.astype(BF16)
    return result.reshape(drafts, requests, -1)


def solution(mesh):
    return jax.shard_map(
        on_device,
        mesh=mesh,
        in_specs=(
            P(None, "inst", "tp", None),
            P(None, "inst", "tp", None),
            P(None, "inst", "tp", None),
            P("inst", "tp", None, None),
            P("inst", "tp", None, None),
            P("inst"),
            P("inst"),
            P("tp", None),
        ),
        out_specs=P(None, "inst", "tp"),
        check_vma=False,
    )
```

```python
import functools
import math

import jax
import jax.numpy as jnp
from jax import lax
from jax.experimental import pallas as pl
from jax.experimental.pallas import tpu as pltpu
from jax.sharding import PartitionSpec as P

NEG = -1e30
F32 = jnp.float32
BF16 = jnp.bfloat16
META = 8
EARLY = 512


def in_hbm(x):
    return pltpu.with_memory_space_constraint(x, pltpu.HBM)


def draft_block(drafts, q, k_ref, v_ref, out_ref, stat_ref):
    requests, rows, head = q.shape
    group = rows // drafts
    tall = requests * rows
    wide = k_ref.shape[0]
    s = lax.dot_general(
        k_ref[...], q.reshape(tall, head), (((1,), (1,)), ((), ())), preferred_element_type=F32
    )
    key = lax.broadcasted_iota(jnp.int32, (wide, tall), 0)
    row = lax.broadcasted_iota(jnp.int32, (wide, tall), 1)
    request_bits, rows_bits, group_bits = (n.bit_length() - 1 for n in (requests, rows, group))
    own = lax.shift_right_logical(row, rows_bits) == (key & (requests - 1))
    drafted = lax.shift_right_logical(row & (rows - 1), group_bits)
    valid = own & (lax.shift_right_logical(key, request_bits) <= drafted)
    s = jnp.where(valid, s * head ** (-0.5), NEG)
    peak = jnp.max(s, axis=0, keepdims=True)
    weight = jnp.exp(s - peak)
    total = jnp.sum(weight, axis=0, keepdims=True)
    out_ref[...] = lax.dot_general(
        weight.astype(BF16), v_ref[...], (((0,), (0,)), ((), ())), preferred_element_type=F32
    ).reshape(requests, rows, head)
    for r in range(requests):
        start = r * rows // head * head
        for n, x in enumerate((peak, total)):
            piece = x[:, start : start + head]
            if r * rows > start:
                piece = pltpu.roll(piece, head - (r * rows - start), 1)
            stat_ref[n, r : r + 1, :] = piece


def weight_copy(w_hbm, w_ref, start, stop, sem):
    here = pl.ds(start, stop - start)
    return pltpu.make_async_copy(w_hbm.at[here], w_ref.at[here], sem)


def prepare_kernel(
    shifts, table_hbm, length_hbm, queries_hbm, w_hbm,
    out_ref, place_ref, q_ref, w_ref,
    table_ref, length_ref, queries_ref, meta_ref, count_ref, sems, w_sem,
):
    drafts, requests, group, head = queries_ref.shape
    lenders = out_ref.shape[0]
    rows = drafts * group
    entries = table_ref.shape[0]
    each = entries // lenders
    blocks = entries // requests
    pool_bits, each_bits, block_bits = shifts
    pairs = ((table_hbm, table_ref), (length_hbm, length_ref), (queries_hbm, queries_ref))
    copies = [pltpu.make_async_copy(a, b, sems.at[i]) for i, (a, b) in enumerate(pairs)]
    for copy in copies:
        copy.start()
    for i in range(lenders):
        count_ref[i] = 0
    first_half = lax.broadcasted_iota(jnp.int32, (1, head), 1) < head // 2
    copies[0].wait()
    copies[1].wait()
    for e in range(entries):
        slot = table_ref[e]
        lender = lax.shift_right_logical(slot, pool_bits)
        j = count_ref[lender]
        count_ref[lender] = j + 1
        place_ref[e] = lender * each + j
        limit = jnp.clip(length_ref[e // blocks] - (e % blocks << block_bits), 0, 1 << block_bits)
        inner = slot & ((1 << pool_bits) - 1)
        meta_ref[lender, pl.ds(j, 1), :] = jnp.where(first_half, inner, limit).astype(F32)
    copies[2].wait()
    for r in range(requests):
        q = jnp.concatenate([queries_ref[d, r] for d in range(drafts)], axis=0)
        q_ref[r] = q
        for b in range(blocks):
            place = place_ref[r * blocks + b]
            lender = lax.shift_right_logical(place, each_bits)
            start = pl.multiple_of((place & (each - 1)) * rows, rows)
            out_ref[lender, pl.ds(start, rows), :] = q
    out_ref[:, each * rows :, :] = meta_ref[...].astype(BF16)

    @pl.when(lax.axis_index("tp") & 1 == 0)
    def _():
        copy = weight_copy(w_hbm, w_ref, 0, EARLY, w_sem)
        copy.start()
        copy.wait()


def prepare(table, lengths, queries, w, block):
    drafts, requests, group, head = queries.shape
    rows = drafts * group
    entries = table.shape[0]
    lenders = lax.axis_size("inst")
    each = entries // lenders
    shifts = tuple(n.bit_length() - 1 for n in (entries, each, block))
    vmem, smem = pl.BlockSpec(memory_space=pltpu.VMEM), pl.BlockSpec(memory_space=pltpu.SMEM)
    return pl.pallas_call(
        functools.partial(prepare_kernel, shifts),
        in_specs=[pl.BlockSpec(memory_space=pltpu.HBM)] * 4,
        out_specs=[vmem, smem, vmem, vmem],
        out_shape=[
            jax.ShapeDtypeStruct((lenders, each * rows + META, head), BF16),
            jax.ShapeDtypeStruct((entries,), jnp.int32),
            jax.ShapeDtypeStruct((requests, rows, head), BF16),
            pltpu.VMEM(w.shape, BF16),
        ],
        scratch_shapes=[
            pltpu.SMEM(table.shape, jnp.int32),
            pltpu.SMEM(lengths.shape, jnp.int32),
            pltpu.VMEM(queries.shape, BF16),
            pltpu.VMEM((lenders, META, head), F32),
            pltpu.SMEM((lenders,), jnp.int32),
            pltpu.SemaphoreType.DMA((3,)),
            pltpu.SemaphoreType.DMA,
        ],
        compiler_params=pltpu.CompilerParams(vmem_limit_bytes=8 * 1024 * 1024),
        cost_estimate=pl.CostEstimate(
            flops=2 * 10**10, bytes_accessed=64 * 1024 * 1024, transcendentals=10**7
        ),
        name="prepare",
    )(*(in_hbm(x) for x in (table, lengths, queries, w)))


def attend_kernel(
    drafts, ahead, behind, q_ref, k_ref, v_ref, own_ref, new_k_ref, new_v_ref, w_hbm, w_in,
    out_ref, fresh_ref, stat_ref, w_ref, number_ref, info_ref, sem, w_sem,
):
    others = weight_copy(w_hbm, w_ref, EARLY, w_ref.shape[0], w_sem)
    others.start()

    block, head = k_ref.shape[1:]
    rows = own_ref.shape[1]
    lenders = out_ref.shape[0]
    each = (out_ref.shape[1] - META) // rows
    entries = lenders * each
    scale = head ** (-0.5)
    fast = scale * math.log2(math.e)

    lane = lax.broadcasted_iota(jnp.int32, (META, head), 1)
    row = lax.broadcasted_iota(jnp.int32, (META, head), 0)
    for n in range(lenders):
        meta = jnp.where(lane & (head // 2 - 1) == row, q_ref[n, each * rows :, :].astype(F32), 0.0)
        number_ref[n : n + 1, :] = jnp.sum(meta, axis=0, keepdims=True).astype(jnp.int32)
    copy = pltpu.make_async_copy(number_ref, info_ref, sem)
    copy.start()
    copy.wait()

    token = lax.broadcasted_iota(jnp.int32, (8, block), 1)
    column = lax.broadcasted_iota(jnp.int32, (rows, head), 1)
    slot = [info_ref[i // each, i % each] for i in range(entries)]
    limit = [info_ref[i // each, head // 2 + i % each] for i in range(entries)]

    def here(i):
        return i // each, pl.ds(i % each * rows, rows), slice(None)

    scores, soft, outs = {}, {}, {}
    peaks = jnp.zeros((rows, head), F32)
    totals = jnp.ones((rows, head), F32)
    for i in range(-ahead, entries + 2 * behind):
        if i == 32:
            draft_block(drafts, own_ref[...], new_k_ref, new_v_ref, fresh_ref, stat_ref)
        if i + ahead < entries:
            n = i + ahead
            scores[n] = lax.dot_general(
                q_ref[here(n)],
                k_ref[slot[n]],
                (((1,), (1,)), ((), ())),
                preferred_element_type=F32,
            )
        if 0 <= i < entries:
            bias = jnp.where(token < limit[i], 0.0, NEG)
            s = scores.pop(i).reshape(rows // 8, 8, block) + bias[None]
            s = s.reshape(rows, block)
            peak = jnp.max(s, axis=1, keepdims=True)
            weight = jnp.exp2((s - peak) * fast)
            soft[i] = peak, jnp.sum(weight, axis=1, keepdims=True), weight.astype(BF16)
        if 0 <= i - behind < entries:
            n = i - behind
            outs[n] = jnp.dot(soft[n][2], v_ref[slot[n]], preferred_element_type=F32)
        if 0 <= i - 2 * behind < entries:
            n = i - 2 * behind
            peak, total, _ = soft.pop(n)
            out_ref[here(n)] = (outs.pop(n) * (1.0 / total)).astype(BF16)
            peaks = jnp.where(column == n, peak, peaks)
            totals = jnp.where(column == n, total, totals)

    x = peaks * scale + jnp.log(totals)
    hi = x.astype(BF16).astype(F32)
    rest = x - hi
    mid = rest.astype(BF16).astype(F32)
    low = rest - mid
    stack = jnp.concatenate([hi, mid, low, jnp.zeros((head - 3 * rows, head), F32)], axis=0)
    turned = stack.T
    for i in range(lenders):
        out_ref[i, each * rows :, :] = turned[i * each : (i + 1) * each].astype(BF16)
    others.wait()


def attend(q, keys, values, own, new_keys, new_values, w, w_part, drafts):
    lenders = q.shape[0]
    requests, rows, head = own.shape
    vmem = pl.BlockSpec(memory_space=pltpu.VMEM)
    return pl.pallas_call(
        functools.partial(attend_kernel, drafts, 8, 4),
        in_specs=[vmem] * 6 + [pl.BlockSpec(memory_space=pltpu.HBM), vmem],
        out_specs=[vmem] * 4,
        out_shape=[
            jax.ShapeDtypeStruct(q.shape, BF16),
            jax.ShapeDtypeStruct((requests, rows, head), F32),
            jax.ShapeDtypeStruct((2, requests, head), F32),
            pltpu.VMEM(w.shape, BF16),
        ],
        scratch_shapes=[
            pltpu.VMEM((lenders, head), jnp.int32),
            pltpu.SMEM((lenders, head), jnp.int32),
            pltpu.SemaphoreType.DMA,
            pltpu.SemaphoreType.DMA,
        ],
        input_output_aliases={7: 3},
        compiler_params=pltpu.CompilerParams(vmem_limit_bytes=8 * 1024 * 1024),
        name="attend",
    )(q, keys, values, own, new_keys, new_values, in_hbm(w), w_part)


def combine_kernel(
    drafts, place_ref, got_ref, fresh_ref, stat_ref, w_hbm, w_in,
    send_ref, att_ref, w_ref, arrived_ref, own_ref, rows_ref, w_sem,
):
    first = weight_copy(w_hbm, w_ref, 0, EARLY, w_sem)

    @pl.when(lax.axis_index("tp") & 1 == 1)
    def _():
        first.start()

    requests, rows, head = fresh_ref.shape
    lenders = got_ref.shape[0]
    entries = place_ref.shape[0]
    each = entries // lenders
    each_bits = each.bit_length() - 1
    blocks = entries // requests
    group = rows // drafts

    for i in range(lenders):
        arrived_ref[i * each : (i + 1) * each, :] = got_ref[i, each * rows :, :].astype(F32)
    for e in range(entries):
        own_ref[e : e + 1, :] = arrived_ref[pl.ds(place_ref[e], 1), :]
    x = own_ref[...]
    lse = x + pltpu.roll(x, head - rows, 1) + pltpu.roll(x, head - 2 * rows, 1)
    lse = lse.reshape(requests, blocks, head)
    fresh_peak = stat_ref[0]
    top = jnp.maximum(jnp.max(lse, axis=1), fresh_peak)
    weight = jnp.exp(lse - top[:, None])
    fresh_weight = jnp.exp(fresh_peak - top)
    part = 1.0 / (jnp.sum(weight, axis=1) + stat_ref[1] * fresh_weight)
    lane = lax.broadcasted_iota(jnp.int32, (entries, head), 1)
    weight = jnp.where(lane < rows, (weight * part[:, None]).reshape(entries, head), 0.0)
    fresh_weight = fresh_weight * part
    fresh_weight = jnp.concatenate(
        [fresh_weight, jnp.zeros((head - requests, head), F32)], axis=0
    ).T
    beside = head // rows
    rows_bits = rows.bit_length() - 1
    spread = weight
    for n in range(1, beside):
        spread = spread + pltpu.roll(weight, n * rows, 1)
    lane = lax.broadcasted_iota(jnp.int32, (blocks, head), 1)
    near = lax.broadcasted_iota(jnp.int32, (blocks, head), 0) - lax.shift_right_logical(
        lane, rows_bits
    )
    diagonal = lax.broadcasted_iota(jnp.int32, (rows, head), 0) == (
        lax.broadcasted_iota(jnp.int32, (rows, head), 1) & (rows - 1)
    )
    for r in range(requests):
        mine = spread[r * blocks : (r + 1) * blocks]
        high, low, parts = [], [], []
        for n in range(0, blocks, beside):
            line = jnp.sum(jnp.where(near == n, mine, 0.0), axis=0, keepdims=True)
            square = jnp.where(diagonal, line, 0.0)
            high.append(square.astype(BF16))
            low.append((square - high[-1].astype(F32)).astype(BF16))
        for b in range(blocks):
            place = place_ref[r * blocks + b]
            lender = lax.shift_right_logical(place, each_bits)
            start = pl.multiple_of((place & (each - 1)) * rows, rows)
            parts.append(got_ref[lender, pl.ds(start, rows), :])
        left = jnp.concatenate(
            [jnp.concatenate(high, axis=1), jnp.concatenate(low, axis=1)], axis=0
        )
        both = jnp.dot(left, jnp.concatenate(parts, axis=0), preferred_element_type=F32)
        acc = both[:rows] + both[rows:] + fresh_ref[r] * fresh_weight[:rows, r : r + 1]
        for d in range(drafts):
            rows_ref[pl.ds((d * requests + r) * group, group), :] = acc[
                d * group : (d + 1) * group
            ]
    att = jnp.concatenate(
        [rows_ref[pl.ds(g, drafts * requests, stride=group), :] for g in range(group)], axis=1
    ).astype(BF16)
    att_ref[...] = att

    @pl.when(lax.axis_index("tp") & 1 == 1)
    def _():
        first.wait()

    tile = send_ref.shape[2]
    place_tp = lax.axis_index("tp")
    core = place_tp & 1
    ring = send_ref.shape[0]
    for i in range(send_ref.shape[0]):
        to = ((place_tp >> 1) + i) & (ring - 1)
        here = pl.ds(pl.multiple_of((2 * to + 1 - core) * tile, tile), tile)
        send_ref[i] = jnp.dot(att, w_ref[:, here], preferred_element_type=F32).astype(BF16)


def combine(place, got, fresh, stat, w, w_part, drafts, tp):
    requests, rows, head = fresh.shape
    deep, wide = w.shape
    tile = wide // tp
    tall = drafts * requests
    vmem, smem = pl.BlockSpec(memory_space=pltpu.VMEM), pl.BlockSpec(memory_space=pltpu.SMEM)
    return pl.pallas_call(
        functools.partial(combine_kernel, drafts),
        in_specs=[smem, vmem, vmem, vmem, pl.BlockSpec(memory_space=pltpu.HBM), vmem],
        out_specs=[vmem] * 3,
        out_shape=[
            jax.ShapeDtypeStruct((tp // 2, tall, tile), BF16),
            jax.ShapeDtypeStruct((tall, deep), BF16),
            pltpu.VMEM(w.shape, BF16),
        ],
        scratch_shapes=[
            pltpu.VMEM((place.shape[0], head), F32),
            pltpu.VMEM((place.shape[0], head), F32),
            pltpu.VMEM((requests * rows, head), F32),
            pltpu.SemaphoreType.DMA,
        ],
        input_output_aliases={5: 2},
        compiler_params=pltpu.CompilerParams(vmem_limit_bytes=8 * 1024 * 1024),
        name="combine",
    )(place, got, fresh, stat, in_hbm(w), w_part)


def keep_kernel(att_ref, w_ref, keep_ref):
    tile = keep_ref.shape[2]
    place_tp = lax.axis_index("tp")
    core = place_tp & 1
    ring = keep_ref.shape[0]
    for i in range(ring):
        to = ((place_tp >> 1) + i) & (ring - 1)
        here = pl.ds(pl.multiple_of((2 * to + core) * tile, tile), tile)
        keep_ref[i] = jnp.dot(att_ref[...], w_ref[:, here], preferred_element_type=F32)


def keep_half(att, w, tp):
    deep, wide = w.shape
    tile = wide // tp
    tall = att.shape[0]
    vmem, smem = pl.BlockSpec(memory_space=pltpu.VMEM), pl.BlockSpec(memory_space=pltpu.SMEM)
    return pl.pallas_call(
        keep_kernel,
        in_specs=[vmem, vmem],
        out_specs=vmem,
        out_shape=jax.ShapeDtypeStruct((tp // 2, tall, tile), F32),
        compiler_params=pltpu.CompilerParams(vmem_limit_bytes=8 * 1024 * 1024),
        cost_estimate=pl.CostEstimate(
            flops=tall * deep * wide, bytes_accessed=deep * wide, transcendentals=0
        ),
        name="keep_half",
    )(att, w)


def on_device(
    queries, new_keys, new_values, key_pool, value_pool, block_table, context_len, out_weight
):
    drafts, requests, heads, head = queries.shape
    pool, _, block, _ = key_pool.shape
    tp = lax.axis_size("tp")
    payload, place, own, weight = prepare(block_table, context_len, queries, out_weight, block)
    asked = lax.all_to_all(payload, "inst", 0, 0, tiled=True)
    answer, fresh, stat, weight = attend(
        asked,
        key_pool.reshape(pool, block, head),
        value_pool.reshape(pool, block, head),
        own,
        new_keys.reshape(-1, head),
        new_values.reshape(-1, head),
        out_weight,
        weight,
        drafts,
    )
    got = lax.all_to_all(answer, "inst", 0, 0, tiled=True)

    send, att, weight = combine(place, got, fresh, stat, out_weight, weight, drafts, tp)
    other = lax.ppermute(send, "tp", [(i, i ^ 1) for i in range(tp)])
    keep = keep_half(att, weight, tp)
    ring = tp // 2
    parts = [
        lax.ppermute(
            (keep[n] + other[n].astype(F32)).astype(BF16),
            "tp",
            [(i, (i + 2 * n) % tp) for i in range(tp)],
        )
        for n in (2, 1, 3)
    ]
    total = keep[0] + other[0].astype(F32)
    for part in parts:
        total = total + part.astype(F32)
    result = total.astype(BF16)
    return result.reshape(drafts, requests, -1)


def solution(mesh):
    return jax.shard_map(
        on_device,
        mesh=mesh,
        in_specs=(
            P(None, "inst", "tp", None),
            P(None, "inst", "tp", None),
            P(None, "inst", "tp", None),
            P("inst", "tp", None, None),
            P("inst", "tp", None, None),
            P("inst"),
            P("inst"),
            P("tp", None),
        ),
        out_specs=P(None, "inst", "tp"),
        check_vma=False,
    )
```

```python
import functools
import math

import jax
import jax.numpy as jnp
from jax import lax
from jax.experimental import pallas as pl
from jax.experimental.pallas import tpu as pltpu
from jax.sharding import PartitionSpec as P

NEG = -1e30
F32 = jnp.float32
BF16 = jnp.bfloat16
FAR = 2
REST = (1, 3, 0)
META = 8
EARLY = 512


def in_hbm(x):
    return pltpu.with_memory_space_constraint(x, pltpu.HBM)


def draft_block(drafts, q, k_ref, v_ref, out_ref, stat_ref):
    requests, rows, head = q.shape
    group = rows // drafts
    tall = requests * rows
    wide = k_ref.shape[0]
    s = lax.dot_general(
        k_ref[...], q.reshape(tall, head), (((1,), (1,)), ((), ())), preferred_element_type=F32
    )
    key = lax.broadcasted_iota(jnp.int32, (wide, tall), 0)
    row = lax.broadcasted_iota(jnp.int32, (wide, tall), 1)
    request_bits, rows_bits, group_bits = (n.bit_length() - 1 for n in (requests, rows, group))
    own = lax.shift_right_logical(row, rows_bits) == (key & (requests - 1))
    drafted = lax.shift_right_logical(row & (rows - 1), group_bits)
    valid = own & (lax.shift_right_logical(key, request_bits) <= drafted)
    s = jnp.where(valid, s * head ** (-0.5), NEG)
    yield
    peak = jnp.max(s, axis=0, keepdims=True)
    weight = jnp.exp(s - peak)
    total = jnp.sum(weight, axis=0, keepdims=True)
    yield
    out_ref[...] = lax.dot_general(
        weight.astype(BF16), v_ref[...], (((0,), (0,)), ((), ())), preferred_element_type=F32
    ).reshape(requests, rows, head)
    yield
    for r in range(requests):
        start = r * rows // head * head
        for n, x in enumerate((peak, total)):
            piece = x[:, start : start + head]
            if r * rows > start:
                piece = pltpu.roll(piece, head - (r * rows - start), 1)
            stat_ref[n, r : r + 1, :] = piece
    yield


def weight_copy(w_hbm, w_ref, start, stop, sem):
    here = pl.ds(start, stop - start)
    return pltpu.make_async_copy(w_hbm.at[here], w_ref.at[here], sem)


def prepare_kernel(
    shifts, table_hbm, length_hbm, queries_hbm, w_hbm,
    out_ref, place_hbm, q_ref, w_ref,
    table_ref, length_ref, queries_ref, place_ref, meta_ref, count_ref, sems, w_sem,
):
    drafts, requests, group, head = queries_ref.shape
    lenders = out_ref.shape[0]
    rows = drafts * group
    entries = table_ref.shape[0]
    each = entries // lenders
    blocks = entries // requests
    pool_bits, each_bits, block_bits = shifts
    pairs = ((table_hbm, table_ref), (length_hbm, length_ref), (queries_hbm, queries_ref))
    copies = [pltpu.make_async_copy(a, b, sems.at[i]) for i, (a, b) in enumerate(pairs)]
    for copy in copies:
        copy.start()
    for i in range(lenders):
        count_ref[i] = 0
    first_half = lax.broadcasted_iota(jnp.int32, (1, head), 1) < head // 2
    copies[0].wait()
    copies[1].wait()
    for e in range(entries):
        slot = table_ref[e]
        lender = lax.shift_right_logical(slot, pool_bits)
        j = count_ref[lender]
        count_ref[lender] = j + 1
        place_ref[e] = lender * each + j
        limit = jnp.clip(length_ref[e // blocks] - (e % blocks << block_bits), 0, 1 << block_bits)
        inner = slot & ((1 << pool_bits) - 1)
        meta_ref[lender, pl.ds(j, 1), :] = jnp.where(first_half, inner, limit).astype(F32)
    places = pltpu.make_async_copy(place_ref, place_hbm, sems.at[3])
    places.start()
    copies[2].wait()
    for r in range(requests):
        q = jnp.concatenate([queries_ref[d, r] for d in range(drafts)], axis=0)
        q_ref[r] = q
        for b in range(blocks):
            place = place_ref[r * blocks + b]
            lender = lax.shift_right_logical(place, each_bits)
            start = pl.multiple_of((place & (each - 1)) * rows, rows)
            out_ref[lender, pl.ds(start, rows), :] = q
    out_ref[:, each * rows :, :] = meta_ref[...].astype(BF16)
    places.wait()

    @pl.when(lax.axis_index("tp") & 1 == 0)
    def _():
        copy = weight_copy(w_hbm, w_ref, 0, EARLY, w_sem)
        copy.start()
        copy.wait()


def prepare(table, lengths, queries, w, block):
    drafts, requests, group, head = queries.shape
    rows = drafts * group
    entries = table.shape[0]
    lenders = lax.axis_size("inst")
    each = entries // lenders
    shifts = tuple(n.bit_length() - 1 for n in (entries, each, block))
    vmem = pl.BlockSpec(memory_space=pltpu.VMEM)
    return pl.pallas_call(
        functools.partial(prepare_kernel, shifts),
        in_specs=[pl.BlockSpec(memory_space=pltpu.HBM)] * 4,
        out_specs=[vmem, pl.BlockSpec(memory_space=pltpu.HBM), vmem, vmem],
        out_shape=[
            jax.ShapeDtypeStruct((lenders, each * rows + META, head), BF16),
            pltpu.HBM((entries,), jnp.int32),
            jax.ShapeDtypeStruct((requests, rows, head), BF16),
            pltpu.VMEM(w.shape, BF16),
        ],
        scratch_shapes=[
            pltpu.SMEM(table.shape, jnp.int32),
            pltpu.SMEM(lengths.shape, jnp.int32),
            pltpu.VMEM(queries.shape, BF16),
            pltpu.SMEM((entries,), jnp.int32),
            pltpu.VMEM((lenders, META, head), F32),
            pltpu.SMEM((lenders,), jnp.int32),
            pltpu.SemaphoreType.DMA((4,)),
            pltpu.SemaphoreType.DMA,
        ],
        compiler_params=pltpu.CompilerParams(vmem_limit_bytes=8 * 1024 * 1024),
        cost_estimate=pl.CostEstimate(
            flops=2 * 10**10, bytes_accessed=64 * 1024 * 1024, transcendentals=10**7
        ),
        name="prepare",
    )(*(in_hbm(x) for x in (table, lengths, queries, w)))


def attend_kernel(
    drafts, ahead, behind, q_ref, k_ref, v_ref, own_ref, new_k_ref, new_v_ref, w_hbm, w_in,
    out_ref, fresh_ref, stat_ref, w_ref, number_ref, info_ref, sem, w_sem,
):
    others = weight_copy(w_hbm, w_ref, EARLY, w_ref.shape[0], w_sem)
    others.start()

    block, head = k_ref.shape[1:]
    rows = own_ref.shape[1]
    lenders = out_ref.shape[0]
    each = (out_ref.shape[1] - META) // rows
    entries = lenders * each
    scale = head ** (-0.5)
    fast = scale * math.log2(math.e)

    lane = lax.broadcasted_iota(jnp.int32, (META, head), 1)
    row = lax.broadcasted_iota(jnp.int32, (META, head), 0)
    for n in range(lenders):
        meta = jnp.where(lane & (head // 2 - 1) == row, q_ref[n, each * rows :, :].astype(F32), 0.0)
        number_ref[n : n + 1, :] = jnp.sum(meta, axis=0, keepdims=True).astype(jnp.int32)
    copy = pltpu.make_async_copy(number_ref, info_ref, sem)
    copy.start()
    copy.wait()

    token = lax.broadcasted_iota(jnp.int32, (8, block), 1)
    column = lax.broadcasted_iota(jnp.int32, (rows, head), 1)
    slot = [info_ref[i // each, i % each] for i in range(entries)]
    limit = [info_ref[i // each, head // 2 + i % each] for i in range(entries)]

    def here(i):
        return i // each, pl.ds(i % each * rows, rows), slice(None)

    draft = draft_block(drafts, own_ref[...], new_k_ref, new_v_ref, fresh_ref, stat_ref)
    scores, soft, outs = {}, {}, {}
    peaks = jnp.zeros((rows, head), F32)
    totals = jnp.ones((rows, head), F32)
    for i in range(-ahead, entries + 2 * behind):
        if i in (16, 28, 40, 52):
            next(draft)
        if i + ahead < entries:
            n = i + ahead
            scores[n] = lax.dot_general(
                q_ref[here(n)],
                k_ref[slot[n]],
                (((1,), (1,)), ((), ())),
                preferred_element_type=F32,
            )
        if 0 <= i < entries:
            bias = jnp.where(token < limit[i], 0.0, NEG)
            s = scores.pop(i).reshape(rows // 8, 8, block) + bias[None]
            s = s.reshape(rows, block)
            peak = jnp.max(s, axis=1, keepdims=True)
            weight = jnp.exp2((s - peak) * fast)
            soft[i] = peak, jnp.sum(weight, axis=1, keepdims=True), weight.astype(BF16)
        if 0 <= i - behind < entries:
            n = i - behind
            outs[n] = jnp.dot(soft[n][2], v_ref[slot[n]], preferred_element_type=F32)
        if 0 <= i - 2 * behind < entries:
            n = i - 2 * behind
            peak, total, _ = soft.pop(n)
            out_ref[here(n)] = (outs.pop(n) * (1.0 / total)).astype(BF16)
            peaks = jnp.where(column == n, peak, peaks)
            totals = jnp.where(column == n, total, totals)

    x = peaks * scale + jnp.log(totals)
    hi = x.astype(BF16).astype(F32)
    rest = x - hi
    mid = rest.astype(BF16).astype(F32)
    low = rest - mid
    stack = jnp.concatenate([hi, mid, low, jnp.zeros((head - 3 * rows, head), F32)], axis=0)
    turned = stack.T
    for i in range(lenders):
        out_ref[i, each * rows :, :] = turned[i * each : (i + 1) * each].astype(BF16)
    others.wait()


def attend(q, keys, values, own, new_keys, new_values, w, w_part, drafts):
    lenders = q.shape[0]
    requests, rows, head = own.shape
    vmem = pl.BlockSpec(memory_space=pltpu.VMEM)
    return pl.pallas_call(
        functools.partial(attend_kernel, drafts, 8, 4),
        in_specs=[vmem] * 6 + [pl.BlockSpec(memory_space=pltpu.HBM), vmem],
        out_specs=[vmem] * 4,
        out_shape=[
            jax.ShapeDtypeStruct(q.shape, BF16),
            jax.ShapeDtypeStruct((requests, rows, head), F32),
            jax.ShapeDtypeStruct((2, requests, head), F32),
            pltpu.VMEM(w.shape, BF16),
        ],
        scratch_shapes=[
            pltpu.VMEM((lenders, head), jnp.int32),
            pltpu.SMEM((lenders, head), jnp.int32),
            pltpu.SemaphoreType.DMA,
            pltpu.SemaphoreType.DMA,
        ],
        input_output_aliases={7: 3},
        compiler_params=pltpu.CompilerParams(vmem_limit_bytes=8 * 1024 * 1024),
        name="attend",
    )(q, keys, values, own, new_keys, new_values, in_hbm(w), w_part)


def project_to(steps, other, att_ref, w_ref, out_ref):
    place = lax.axis_index("tp")
    core = 1 - (place & 1) if other else place & 1
    tile = out_ref.shape[2]
    ring = w_ref.shape[1] // tile // 2
    for i, step in enumerate(steps):
        to = ((place >> 1) + step) & (ring - 1)
        here = pl.ds(pl.multiple_of((2 * to + core) * tile, tile), tile)
        out = jnp.dot(att_ref[...], w_ref[:, here], preferred_element_type=F32)
        out_ref[i] = out.astype(out_ref.dtype)


def combine_kernel(
    drafts, place_ref, got_ref, fresh_ref, stat_ref, w_hbm, w_in,
    far_ref, send_ref, att_ref, w_ref, arrived_ref, own_ref, rows_ref, w_sem,
):
    first = weight_copy(w_hbm, w_ref, 0, EARLY, w_sem)

    @pl.when(lax.axis_index("tp") & 1 == 1)
    def _():
        first.start()

    requests, rows, head = fresh_ref.shape
    lenders = got_ref.shape[0]
    entries = place_ref.shape[0]
    each = entries // lenders
    each_bits = each.bit_length() - 1
    blocks = entries // requests
    group = rows // drafts

    for i in range(lenders):
        arrived_ref[i * each : (i + 1) * each, :] = got_ref[i, each * rows :, :].astype(F32)
    for e in range(entries):
        own_ref[e : e + 1, :] = arrived_ref[pl.ds(place_ref[e], 1), :]
    x = own_ref[...]
    lse = x + pltpu.roll(x, head - rows, 1) + pltpu.roll(x, head - 2 * rows, 1)
    lse = lse.reshape(requests, blocks, head)
    fresh_peak = stat_ref[0]
    top = jnp.maximum(jnp.max(lse, axis=1), fresh_peak)
    weight = jnp.exp(lse - top[:, None])
    fresh_weight = jnp.exp(fresh_peak - top)
    part = 1.0 / (jnp.sum(weight, axis=1) + stat_ref[1] * fresh_weight)
    lane = lax.broadcasted_iota(jnp.int32, (entries, head), 1)
    weight = jnp.where(lane < rows, (weight * part[:, None]).reshape(entries, head), 0.0)
    fresh_weight = fresh_weight * part
    fresh_weight = jnp.concatenate(
        [fresh_weight, jnp.zeros((head - requests, head), F32)], axis=0
    ).T
    beside = head // rows
    rows_bits = rows.bit_length() - 1
    spread = weight
    for n in range(1, beside):
        spread = spread + pltpu.roll(weight, n * rows, 1)
    lane = lax.broadcasted_iota(jnp.int32, (blocks, head), 1)
    near = lax.broadcasted_iota(jnp.int32, (blocks, head), 0) - lax.shift_right_logical(
        lane, rows_bits
    )
    diagonal = lax.broadcasted_iota(jnp.int32, (rows, head), 0) == (
        lax.broadcasted_iota(jnp.int32, (rows, head), 1) & (rows - 1)
    )
    for r in range(requests):
        mine = spread[r * blocks : (r + 1) * blocks]
        high, low, parts = [], [], []
        for n in range(0, blocks, beside):
            line = jnp.sum(jnp.where(near == n, mine, 0.0), axis=0, keepdims=True)
            square = jnp.where(diagonal, line, 0.0)
            high.append(square.astype(BF16))
            low.append((square - high[-1].astype(F32)).astype(BF16))
        for b in range(blocks):
            place = place_ref[r * blocks + b]
            lender = lax.shift_right_logical(place, each_bits)
            start = pl.multiple_of((place & (each - 1)) * rows, rows)
            parts.append(got_ref[lender, pl.ds(start, rows), :])
        left = jnp.concatenate(
            [jnp.concatenate(high, axis=1), jnp.concatenate(low, axis=1)], axis=0
        )
        both = jnp.dot(left, jnp.concatenate(parts, axis=0), preferred_element_type=F32)
        acc = both[:rows] + both[rows:] + fresh_ref[r] * fresh_weight[:rows, r : r + 1]
        for d in range(drafts):
            rows_ref[pl.ds((d * requests + r) * group, group), :] = acc[
                d * group : (d + 1) * group
            ]
    att = jnp.concatenate(
        [rows_ref[pl.ds(g, drafts * requests, stride=group), :] for g in range(group)], axis=1
    ).astype(BF16)
    att_ref[...] = att

    @pl.when(lax.axis_index("tp") & 1 == 1)
    def _():
        first.wait()

    project_to((FAR,), True, att_ref, w_ref, far_ref)
    project_to(REST, True, att_ref, w_ref, send_ref)


def combine(place, got, fresh, stat, w, w_part, drafts, tp):
    requests, rows, head = fresh.shape
    deep, wide = w.shape
    tile = wide // tp
    tall = drafts * requests
    vmem, smem = pl.BlockSpec(memory_space=pltpu.VMEM), pl.BlockSpec(memory_space=pltpu.SMEM)
    return pl.pallas_call(
        functools.partial(combine_kernel, drafts),
        in_specs=[smem, vmem, vmem, vmem, pl.BlockSpec(memory_space=pltpu.HBM), vmem],
        out_specs=[vmem] * 4,
        out_shape=[
            jax.ShapeDtypeStruct((1, tall, tile), BF16),
            jax.ShapeDtypeStruct((len(REST), tall, tile), BF16),
            jax.ShapeDtypeStruct((tall, deep), BF16),
            pltpu.VMEM(w.shape, BF16),
        ],
        scratch_shapes=[
            pltpu.VMEM((place.shape[0], head), F32),
            pltpu.VMEM((place.shape[0], head), F32),
            pltpu.VMEM((requests * rows, head), F32),
            pltpu.SemaphoreType.DMA,
        ],
        input_output_aliases={5: 3},
        compiler_params=pltpu.CompilerParams(vmem_limit_bytes=8 * 1024 * 1024),
        name="combine",
    )(place, got, fresh, stat, in_hbm(w), w_part)


def keep(steps, att, w, tp):
    deep, wide = w.shape
    tile = wide // tp
    tall = att.shape[0]
    vmem = pl.BlockSpec(memory_space=pltpu.VMEM)
    return pl.pallas_call(
        functools.partial(project_to, steps, False),
        in_specs=[vmem, vmem],
        out_specs=vmem,
        out_shape=jax.ShapeDtypeStruct((len(steps), tall, tile), F32),
        compiler_params=pltpu.CompilerParams(vmem_limit_bytes=8 * 1024 * 1024),
        cost_estimate=pl.CostEstimate(
            flops=2 * tall * deep * tile * len(steps),
            bytes_accessed=2 * deep * tile * len(steps),
            transcendentals=0,
        ),
        name="keep",
    )(att, w)


def on_device(
    queries, new_keys, new_values, key_pool, value_pool, block_table, context_len, out_weight
):
    drafts, requests, heads, head = queries.shape
    pool, _, block, _ = key_pool.shape
    tp = lax.axis_size("tp")
    payload, place, own, weight = prepare(block_table, context_len, queries, out_weight, block)
    asked = lax.all_to_all(payload, "inst", 0, 0, tiled=True)
    answer, fresh, stat, weight = attend(
        asked,
        key_pool.reshape(pool, block, head),
        value_pool.reshape(pool, block, head),
        own,
        new_keys.reshape(-1, head),
        new_values.reshape(-1, head),
        out_weight,
        weight,
        drafts,
    )
    got = lax.all_to_all(answer, "inst", 0, 0, tiled=True)

    far, send, att, weight = combine(place, got, fresh, stat, out_weight, weight, drafts, tp)
    swap = [(i, i ^ 1) for i in range(tp)]

    def along(pair, step):
        return lax.ppermute(pair.astype(BF16), "tp", [(i, (i + 2 * step) % tp) for i in range(tp)])

    other_far = lax.ppermute(far, "tp", swap)
    other = lax.ppermute(send, "tp", swap)
    pair = keep((FAR,), att, weight, tp)[0] + other_far[0].astype(F32)
    parts = [along(pair, FAR)]
    att, _ = lax.optimization_barrier((att, pair))
    kept = keep(REST, att, weight, tp)
    pairs = [kept[n] + other[n].astype(F32) for n in range(len(REST))]
    parts += [along(pairs[n], REST[n]) for n in range(2)]
    total = pairs[2]
    for part in parts:
        total = total + part.astype(F32)
    result = total.astype(BF16)
    return result.reshape(drafts, requests, -1)


def solution(mesh):
    return jax.shard_map(
        on_device,
        mesh=mesh,
        in_specs=(
            P(None, "inst", "tp", None),
            P(None, "inst", "tp", None),
            P(None, "inst", "tp", None),
            P("inst", "tp", None, None),
            P("inst", "tp", None, None),
            P("inst"),
            P("inst"),
            P("tp", None),
        ),
        out_specs=P(None, "inst", "tp"),
        check_vma=False,
    )
```

```python
import functools
import math

import jax
import jax.numpy as jnp
from jax import lax
from jax.experimental import pallas as pl
from jax.experimental.pallas import tpu as pltpu
from jax.sharding import PartitionSpec as P

NEG = -1e30
F32 = jnp.float32
BF16 = jnp.bfloat16
FAR = 2
REST = (1, 3, 0)
META = 8
EARLY = 512


def in_hbm(x):
    return pltpu.with_memory_space_constraint(x, pltpu.HBM)


def draft_block(drafts, q, k_ref, v_ref, out_ref, stat_ref):
    requests, rows, head = q.shape
    group = rows // drafts
    tall = requests * rows
    wide = k_ref.shape[0]
    s = lax.dot_general(
        k_ref[...], q.reshape(tall, head), (((1,), (1,)), ((), ())), preferred_element_type=F32
    )
    key = lax.broadcasted_iota(jnp.int32, (wide, tall), 0)
    row = lax.broadcasted_iota(jnp.int32, (wide, tall), 1)
    request_bits, rows_bits, group_bits = (n.bit_length() - 1 for n in (requests, rows, group))
    own = lax.shift_right_logical(row, rows_bits) == (key & (requests - 1))
    drafted = lax.shift_right_logical(row & (rows - 1), group_bits)
    valid = own & (lax.shift_right_logical(key, request_bits) <= drafted)
    s = jnp.where(valid, s * head ** (-0.5), NEG)
    yield
    peak = jnp.max(s, axis=0, keepdims=True)
    weight = jnp.exp(s - peak)
    total = jnp.sum(weight, axis=0, keepdims=True)
    yield
    out_ref[...] = lax.dot_general(
        weight.astype(BF16), v_ref[...], (((0,), (0,)), ((), ())), preferred_element_type=F32
    ).reshape(requests, rows, head)
    yield
    for r in range(requests):
        start = r * rows // head * head
        for n, x in enumerate((peak, total)):
            piece = x[:, start : start + head]
            if r * rows > start:
                piece = pltpu.roll(piece, head - (r * rows - start), 1)
            stat_ref[n, r : r + 1, :] = piece
    yield


def weight_copy(w_hbm, w_ref, start, stop, sem):
    here = pl.ds(start, stop - start)
    return pltpu.make_async_copy(w_hbm.at[here], w_ref.at[here], sem)


def prepare_kernel(
    shifts, table_hbm, length_hbm, queries_hbm, k_hbm, v_hbm, w_hbm,
    out_ref, place_hbm, q_ref, w_ref, fresh_ref, stat_ref, k_ref, v_ref,
    table_ref, length_ref, queries_ref, place_ref, meta_ref, count_ref, sems, w_sem,
):
    drafts, requests, group, head = queries_ref.shape
    lenders = out_ref.shape[0]
    rows = drafts * group
    entries = table_ref.shape[0]
    each = entries // lenders
    blocks = entries // requests
    pool_bits, each_bits, block_bits = shifts
    pairs = ((table_hbm, table_ref), (length_hbm, length_ref), (queries_hbm, queries_ref))
    copies = [pltpu.make_async_copy(a, b, sems.at[i]) for i, (a, b) in enumerate(pairs)]
    for copy in copies:
        copy.start()
    for i in range(lenders):
        count_ref[i] = 0
    first_half = lax.broadcasted_iota(jnp.int32, (1, head), 1) < head // 2
    copies[0].wait()
    copies[1].wait()
    for e in range(entries):
        slot = table_ref[e]
        lender = lax.shift_right_logical(slot, pool_bits)
        j = count_ref[lender]
        count_ref[lender] = j + 1
        place_ref[e] = lender * each + j
        limit = jnp.clip(length_ref[e // blocks] - (e % blocks << block_bits), 0, 1 << block_bits)
        inner = slot & ((1 << pool_bits) - 1)
        meta_ref[lender, pl.ds(j, 1), :] = jnp.where(first_half, inner, limit).astype(F32)
    places = pltpu.make_async_copy(place_ref, place_hbm, sems.at[3])
    places.start()
    copies[2].wait()
    for r in range(requests):
        q = jnp.concatenate([queries_ref[d, r] for d in range(drafts)], axis=0)
        q_ref[r] = q
        for b in range(blocks):
            place = place_ref[r * blocks + b]
            lender = lax.shift_right_logical(place, each_bits)
            start = pl.multiple_of((place & (each - 1)) * rows, rows)
            out_ref[lender, pl.ds(start, rows), :] = q
    out_ref[:, each * rows :, :] = meta_ref[...].astype(BF16)
    places.wait()

    @pl.when(lax.axis_index("tp") & 1 == 0)
    def _():
        copy = weight_copy(w_hbm, w_ref, 0, EARLY, w_sem)
        copy.start()
        news = [
            pltpu.make_async_copy(k_hbm, k_ref, sems.at[4]),
            pltpu.make_async_copy(v_hbm, v_ref, sems.at[5]),
        ]
        for new in news:
            new.start()
        for new in news:
            new.wait()
        for _ in draft_block(drafts, q_ref[...], k_ref, v_ref, fresh_ref, stat_ref):
            pass
        copy.wait()


def prepare(table, lengths, queries, new_keys, new_values, w, block):
    drafts, requests, group, head = queries.shape
    rows = drafts * group
    entries = table.shape[0]
    lenders = lax.axis_size("inst")
    each = entries // lenders
    shifts = tuple(n.bit_length() - 1 for n in (entries, each, block))
    vmem = pl.BlockSpec(memory_space=pltpu.VMEM)
    return pl.pallas_call(
        functools.partial(prepare_kernel, shifts),
        in_specs=[pl.BlockSpec(memory_space=pltpu.HBM)] * 6,
        out_specs=[vmem, pl.BlockSpec(memory_space=pltpu.HBM)] + [vmem] * 4,
        out_shape=[
            jax.ShapeDtypeStruct((lenders, each * rows + META, head), BF16),
            pltpu.HBM((entries,), jnp.int32),
            jax.ShapeDtypeStruct((requests, rows, head), BF16),
            pltpu.VMEM(w.shape, BF16),
            pltpu.VMEM((requests, rows, head), F32),
            pltpu.VMEM((2, requests, head), F32),
        ],
        scratch_shapes=[
            pltpu.VMEM(new_keys.shape, BF16),
            pltpu.VMEM(new_values.shape, BF16),
            pltpu.SMEM(table.shape, jnp.int32),
            pltpu.SMEM(lengths.shape, jnp.int32),
            pltpu.VMEM(queries.shape, BF16),
            pltpu.SMEM((entries,), jnp.int32),
            pltpu.VMEM((lenders, META, head), F32),
            pltpu.SMEM((lenders,), jnp.int32),
            pltpu.SemaphoreType.DMA((6,)),
            pltpu.SemaphoreType.DMA,
        ],
        compiler_params=pltpu.CompilerParams(vmem_limit_bytes=8 * 1024 * 1024),
        cost_estimate=pl.CostEstimate(
            flops=2 * 10**10, bytes_accessed=64 * 1024 * 1024, transcendentals=10**7
        ),
        name="prepare",
    )(*(in_hbm(x) for x in (table, lengths, queries, new_keys, new_values, w)))


def attend_kernel(
    rows, ahead, behind, q_ref, k_ref, v_ref, w_hbm, w_in,
    out_ref, w_ref, number_ref, info_ref, sem, w_sem,
):
    others = weight_copy(w_hbm, w_ref, EARLY, w_ref.shape[0], w_sem)
    others.start()

    block, head = k_ref.shape[1:]
    lenders = out_ref.shape[0]
    each = (out_ref.shape[1] - META) // rows
    entries = lenders * each
    scale = head ** (-0.5)
    fast = scale * math.log2(math.e)

    lane = lax.broadcasted_iota(jnp.int32, (META, head), 1)
    row = lax.broadcasted_iota(jnp.int32, (META, head), 0)
    for n in range(lenders):
        meta = jnp.where(lane & (head // 2 - 1) == row, q_ref[n, each * rows :, :].astype(F32), 0.0)
        number_ref[n : n + 1, :] = jnp.sum(meta, axis=0, keepdims=True).astype(jnp.int32)
    copy = pltpu.make_async_copy(number_ref, info_ref, sem)
    copy.start()
    copy.wait()

    token = lax.broadcasted_iota(jnp.int32, (8, block), 1)
    column = lax.broadcasted_iota(jnp.int32, (rows, head), 1)
    slot = [info_ref[i // each, i % each] for i in range(entries)]
    limit = [info_ref[i // each, head // 2 + i % each] for i in range(entries)]

    def here(i):
        return i // each, pl.ds(i % each * rows, rows), slice(None)

    scores, soft, outs = {}, {}, {}
    peaks = jnp.zeros((rows, head), F32)
    totals = jnp.ones((rows, head), F32)
    for i in range(-ahead, entries + 2 * behind):
        if i + ahead < entries:
            n = i + ahead
            scores[n] = lax.dot_general(
                q_ref[here(n)],
                k_ref[slot[n]],
                (((1,), (1,)), ((), ())),
                preferred_element_type=F32,
            )
        if 0 <= i < entries:
            bias = jnp.where(token < limit[i], 0.0, NEG)
            s = scores.pop(i).reshape(rows // 8, 8, block) + bias[None]
            s = s.reshape(rows, block)
            peak = jnp.max(s, axis=1, keepdims=True)
            weight = jnp.exp2((s - peak) * fast)
            soft[i] = peak, jnp.sum(weight, axis=1, keepdims=True), weight.astype(BF16)
        if 0 <= i - behind < entries:
            n = i - behind
            outs[n] = jnp.dot(soft[n][2], v_ref[slot[n]], preferred_element_type=F32)
        if 0 <= i - 2 * behind < entries:
            n = i - 2 * behind
            peak, total, _ = soft.pop(n)
            out_ref[here(n)] = (outs.pop(n) * (1.0 / total)).astype(BF16)
            peaks = jnp.where(column == n, peak, peaks)
            totals = jnp.where(column == n, total, totals)

    x = peaks * scale + jnp.log(totals)
    hi = x.astype(BF16).astype(F32)
    rest = x - hi
    mid = rest.astype(BF16).astype(F32)
    low = rest - mid
    stack = jnp.concatenate([hi, mid, low, jnp.zeros((head - 3 * rows, head), F32)], axis=0)
    turned = stack.T
    for i in range(lenders):
        out_ref[i, each * rows :, :] = turned[i * each : (i + 1) * each].astype(BF16)
    others.wait()


def attend(q, keys, values, w, w_part, rows):
    lenders, _, head = q.shape
    vmem = pl.BlockSpec(memory_space=pltpu.VMEM)
    return pl.pallas_call(
        functools.partial(attend_kernel, rows, 8, 4),
        in_specs=[vmem] * 3 + [pl.BlockSpec(memory_space=pltpu.HBM), vmem],
        out_specs=[vmem] * 2,
        out_shape=[
            jax.ShapeDtypeStruct(q.shape, BF16),
            pltpu.VMEM(w.shape, BF16),
        ],
        scratch_shapes=[
            pltpu.VMEM((lenders, head), jnp.int32),
            pltpu.SMEM((lenders, head), jnp.int32),
            pltpu.SemaphoreType.DMA,
            pltpu.SemaphoreType.DMA,
        ],
        input_output_aliases={4: 1},
        compiler_params=pltpu.CompilerParams(vmem_limit_bytes=8 * 1024 * 1024),
        name="attend",
    )(q, keys, values, in_hbm(w), w_part)


def project_to(steps, other, att_ref, w_ref, out_ref):
    place = lax.axis_index("tp")
    core = 1 - (place & 1) if other else place & 1
    tile = out_ref.shape[2]
    ring = w_ref.shape[1] // tile // 2
    for i, step in enumerate(steps):
        to = ((place >> 1) + step) & (ring - 1)
        here = pl.ds(pl.multiple_of((2 * to + core) * tile, tile), tile)
        out = jnp.dot(att_ref[...], w_ref[:, here], preferred_element_type=F32)
        out_ref[i] = out.astype(out_ref.dtype)


def combine_kernel(
    drafts, place_ref, got_ref, fresh_in, stat_in, w_hbm, w_in, q_ref, k_ref, v_ref,
    far_ref, send_ref, att_ref, w_ref, fresh_ref, stat_ref, arrived_ref, own_ref, rows_ref, w_sem,
):
    first = weight_copy(w_hbm, w_ref, 0, EARLY, w_sem)

    @pl.when(lax.axis_index("tp") & 1 == 1)
    def _():
        first.start()
        for _ in draft_block(drafts, q_ref[...], k_ref, v_ref, fresh_ref, stat_ref):
            pass

    requests, rows, head = fresh_ref.shape
    lenders = got_ref.shape[0]
    entries = place_ref.shape[0]
    each = entries // lenders
    each_bits = each.bit_length() - 1
    blocks = entries // requests
    group = rows // drafts

    for i in range(lenders):
        arrived_ref[i * each : (i + 1) * each, :] = got_ref[i, each * rows :, :].astype(F32)
    for e in range(entries):
        own_ref[e : e + 1, :] = arrived_ref[pl.ds(place_ref[e], 1), :]
    x = own_ref[...]
    lse = x + pltpu.roll(x, head - rows, 1) + pltpu.roll(x, head - 2 * rows, 1)
    lse = lse.reshape(requests, blocks, head)
    fresh_peak = stat_ref[0]
    top = jnp.maximum(jnp.max(lse, axis=1), fresh_peak)
    weight = jnp.exp(lse - top[:, None])
    fresh_weight = jnp.exp(fresh_peak - top)
    part = 1.0 / (jnp.sum(weight, axis=1) + stat_ref[1] * fresh_weight)
    lane = lax.broadcasted_iota(jnp.int32, (entries, head), 1)
    weight = jnp.where(lane < rows, (weight * part[:, None]).reshape(entries, head), 0.0)
    fresh_weight = fresh_weight * part
    fresh_weight = jnp.concatenate(
        [fresh_weight, jnp.zeros((head - requests, head), F32)], axis=0
    ).T
    beside = head // rows
    rows_bits = rows.bit_length() - 1
    spread = weight
    for n in range(1, beside):
        spread = spread + pltpu.roll(weight, n * rows, 1)
    lane = lax.broadcasted_iota(jnp.int32, (blocks, head), 1)
    near = lax.broadcasted_iota(jnp.int32, (blocks, head), 0) - lax.shift_right_logical(
        lane, rows_bits
    )
    diagonal = lax.broadcasted_iota(jnp.int32, (rows, head), 0) == (
        lax.broadcasted_iota(jnp.int32, (rows, head), 1) & (rows - 1)
    )
    for r in range(requests):
        mine = spread[r * blocks : (r + 1) * blocks]
        high, low, parts = [], [], []
        for n in range(0, blocks, beside):
            line = jnp.sum(jnp.where(near == n, mine, 0.0), axis=0, keepdims=True)
            square = jnp.where(diagonal, line, 0.0)
            high.append(square.astype(BF16))
            low.append((square - high[-1].astype(F32)).astype(BF16))
        for b in range(blocks):
            place = place_ref[r * blocks + b]
            lender = lax.shift_right_logical(place, each_bits)
            start = pl.multiple_of((place & (each - 1)) * rows, rows)
            parts.append(got_ref[lender, pl.ds(start, rows), :])
        left = jnp.concatenate(
            [jnp.concatenate(high, axis=1), jnp.concatenate(low, axis=1)], axis=0
        )
        both = jnp.dot(left, jnp.concatenate(parts, axis=0), preferred_element_type=F32)
        acc = both[:rows] + both[rows:] + fresh_ref[r] * fresh_weight[:rows, r : r + 1]
        for d in range(drafts):
            rows_ref[pl.ds((d * requests + r) * group, group), :] = acc[
                d * group : (d + 1) * group
            ]
    att = jnp.concatenate(
        [rows_ref[pl.ds(g, drafts * requests, stride=group), :] for g in range(group)], axis=1
    ).astype(BF16)
    att_ref[...] = att

    @pl.when(lax.axis_index("tp") & 1 == 1)
    def _():
        first.wait()

    project_to((FAR,), True, att_ref, w_ref, far_ref)
    project_to(REST, True, att_ref, w_ref, send_ref)


def combine(place, got, fresh, stat, w, w_part, own, new_keys, new_values, drafts, tp):
    requests, rows, head = fresh.shape
    deep, wide = w.shape
    tile = wide // tp
    tall = drafts * requests
    vmem, smem = pl.BlockSpec(memory_space=pltpu.VMEM), pl.BlockSpec(memory_space=pltpu.SMEM)
    return pl.pallas_call(
        functools.partial(combine_kernel, drafts),
        in_specs=[smem, vmem, vmem, vmem, pl.BlockSpec(memory_space=pltpu.HBM)] + [vmem] * 4,
        out_specs=[vmem] * 6,
        out_shape=[
            jax.ShapeDtypeStruct((1, tall, tile), BF16),
            jax.ShapeDtypeStruct((len(REST), tall, tile), BF16),
            jax.ShapeDtypeStruct((tall, deep), BF16),
            pltpu.VMEM(w.shape, BF16),
            pltpu.VMEM(fresh.shape, F32),
            pltpu.VMEM(stat.shape, F32),
        ],
        scratch_shapes=[
            pltpu.VMEM((place.shape[0], head), F32),
            pltpu.VMEM((place.shape[0], head), F32),
            pltpu.VMEM((requests * rows, head), F32),
            pltpu.SemaphoreType.DMA,
        ],
        input_output_aliases={5: 3, 2: 4, 3: 5},
        compiler_params=pltpu.CompilerParams(vmem_limit_bytes=8 * 1024 * 1024),
        name="combine",
    )(place, got, fresh, stat, in_hbm(w), w_part, own, new_keys, new_values)


def keep(steps, att, w, tp):
    deep, wide = w.shape
    tile = wide // tp
    tall = att.shape[0]
    vmem = pl.BlockSpec(memory_space=pltpu.VMEM)
    return pl.pallas_call(
        functools.partial(project_to, steps, False),
        in_specs=[vmem, vmem],
        out_specs=vmem,
        out_shape=jax.ShapeDtypeStruct((len(steps), tall, tile), F32),
        compiler_params=pltpu.CompilerParams(vmem_limit_bytes=8 * 1024 * 1024),
        cost_estimate=pl.CostEstimate(
            flops=2 * tall * deep * tile * len(steps),
            bytes_accessed=2 * deep * tile * len(steps),
            transcendentals=0,
        ),
        name="keep",
    )(att, w)


def on_device(
    queries, new_keys, new_values, key_pool, value_pool, block_table, context_len, out_weight
):
    drafts, requests, heads, head = queries.shape
    pool, _, block, _ = key_pool.shape
    tp = lax.axis_size("tp")
    new_keys, new_values = new_keys.reshape(-1, head), new_values.reshape(-1, head)
    payload, place, own, weight, fresh, stat = prepare(
        block_table, context_len, queries, new_keys, new_values, out_weight, block
    )
    asked = lax.all_to_all(payload, "inst", 0, 0, tiled=True)
    answer, weight = attend(
        asked,
        key_pool.reshape(pool, block, head),
        value_pool.reshape(pool, block, head),
        out_weight,
        weight,
        drafts * heads,
    )
    got = lax.all_to_all(answer, "inst", 0, 0, tiled=True)

    far, send, att, weight, _, _ = combine(
        place, got, fresh, stat, out_weight, weight, own, new_keys, new_values, drafts, tp
    )
    swap = [(i, i ^ 1) for i in range(tp)]

    def along(pair, step):
        return lax.ppermute(pair.astype(BF16), "tp", [(i, (i + 2 * step) % tp) for i in range(tp)])

    other_far = lax.ppermute(far, "tp", swap)
    other = lax.ppermute(send, "tp", swap)
    pair = keep((FAR,), att, weight, tp)[0] + other_far[0].astype(F32)
    parts = [along(pair, FAR)]
    att, _ = lax.optimization_barrier((att, pair))
    kept = keep(REST, att, weight, tp)
    pairs = [kept[n] + other[n].astype(F32) for n in range(len(REST))]
    parts += [along(pairs[n], REST[n]) for n in range(2)]
    total = pairs[2]
    for part in parts:
        total = total + part.astype(F32)
    result = total.astype(BF16)
    return result.reshape(drafts, requests, -1)


def solution(mesh):
    return jax.shard_map(
        on_device,
        mesh=mesh,
        in_specs=(
            P(None, "inst", "tp", None),
            P(None, "inst", "tp", None),
            P(None, "inst", "tp", None),
            P("inst", "tp", None, None),
            P("inst", "tp", None, None),
            P("inst"),
            P("inst"),
            P("tp", None),
        ),
        out_specs=P(None, "inst", "tp"),
        check_vma=False,
    )
```
